512 devices in a mesh: span: 64 (over x, z), head: 8 (over y, core).
Axes of the slice: x: 4, y: 4, z: 16, core: 2. Of those that a mesh axis runs over, the one named last changes fastest.
Arguments:
- queries: bfloat16 [8192, 3072], P(('span', 'head'))
- keys: bfloat16 [8192, 3072], P(('span', 'head'))
- values: bfloat16 [8192, 3072], P(('span', 'head')), may hold values from -6 to 6
- cache_keys: bfloat16 [8192, 3072], P('span', 'head'), may hold values from -18 to 18
- cache_values: bfloat16 [8192, 3072], P('span', 'head'), may hold values from -6 to 6
- levels: int32 [16], replicated, may hold values from 0 to 15
- first_span: int32 [16], replicated, may hold values from 0 to 7, as said below
- level_gate: float32 [16, 3072], P(None, 'head'), may hold values from 0.1 to 1.9
Outputs:
- attended: bfloat16 [8192, 3072], P(('span', 'head'))
The draws below stay inside these ranges and needn't reach their ends.
Inputs may be any that keep to these rules, and one draw needn't show every extreme that they name: first_span[c] lies between 0 and c // 2.
All inputs are finite; a program needn't handle non-finite values.
Results may differ from the reference program's by a relative error of at most 0.0045.
Values may be sent and summed in bfloat16 or wider, within the bound.
A program may use at most 128 MiB of HBM per device.

```python
import jax
import jax.numpy as jnp
from jax import lax

HD = 128
HEADS = 24
CL = 512
LEVELS = 16
TOKENS = 8192
SPANS = 16
FEAT = 3072


def shared_keys(key):
    return 3.0 * jax.random.normal(key, (TOKENS, FEAT), jnp.float32)


def draw_keys(key, part):
    base = shared_keys(key)
    return jnp.clip(base, -18.0, 18.0).astype(jnp.bfloat16)


def draw_queries(key, part):
    key = jax.random.fold_in(key, 5)
    entries = jax.random.normal(key, (TOKENS, FEAT), jnp.float32)
    return entries.astype(jnp.bfloat16)


def draw_first_span(key, part):
    key = jax.random.fold_in(key, 3)
    span_ids = jnp.arange(SPANS, dtype=jnp.int32)
    drawn = jax.random.randint(key, (SPANS,), 0, span_ids // 2 + 1).astype(jnp.int32)
    return jnp.where(span_ids == SPANS - 1, (SPANS - 1) // 2, drawn).astype(jnp.int32)


def with_ends(array, key, least, high):
    longest = array.shape.index(max(array.shape))
    spots = []
    for shift in (0, 1):
        where = [jax.random.randint(jax.random.fold_in(key, axis), (), 0, length) for axis, length in enumerate(array.shape)]
        where[longest] = (where[longest] + shift) % array.shape[longest]
        spots.append(tuple(where))
    return array.at[spots[0]].set(least).at[spots[1]].set(high)


def block_levels(rng, dims, split, least, largest):
    def one(axis_at, parts):
        draws = jax.random.uniform(jax.random.fold_in(jax.random.fold_in(rng, 6), axis_at), (parts,), jnp.float32, least / len(split), largest / len(split))
        return jnp.repeat(jnp.exp(draws), dims[axis_at] // parts).reshape((-1,) + (1,) * (len(dims) - axis_at - 1))

    loudness = one(*split[0])
    for cut in split[1:]:
        loudness = loudness * one(*cut)
    return loudness


def noise(stream_key, extent, deviation, reach, shards=(), held_as=jnp.bfloat16):
    gain = block_levels(stream_key, extent, shards, -0.22, 0.18) if shards else 1.0
    entries = jax.random.normal(stream_key, extent, jnp.float32) * deviation * gain
    return jnp.minimum(jnp.maximum(entries, -reach), reach).astype(held_as)


def setup_inputs(seed: int = 0) -> dict:
    key_list = jax.random.split(jax.random.key(seed), 9)
    return {
        "queries": draw_queries(jax.random.fold_in(key_list[8], 71), 0),
        "keys": draw_keys(jax.random.fold_in(key_list[8], 71), 0),
        "values": noise(key_list[2], (TOKENS, FEAT), 1.0, 6.0, ((0, 512),)),
        "cache_keys": noise(key_list[3], (TOKENS, FEAT), 3.0, 18.0, ((0, 64), (1, 8))),
        "cache_values": noise(key_list[4], (TOKENS, FEAT), 1.0, 6.0, ((0, 64), (1, 8))),
        "levels": with_ends(jax.random.randint(key_list[5], (SPANS,), 0, LEVELS), jax.random.fold_in(key_list[5], 1), 0, LEVELS - 1).astype(jnp.int32),
        "first_span": draw_first_span(jax.random.fold_in(key_list[8], 71), 0),
        "level_gate": jnp.clip(1.0 + 0.18 * jax.random.normal(key_list[7], (LEVELS, FEAT), jnp.float32), 0.1, 1.9),
    }


def head_attend(pieces):
    query_head, key_head, value_head, allowed = pieces
    scores = jnp.dot(query_head, key_head.T) * (HD ** -0.5)
    scores = jnp.where(allowed[None, :], scores, -jnp.inf)
    row_peak = jnp.max(scores, axis=1, keepdims=True)
    weights = jnp.exp(scores - row_peak)
    totals = jnp.sum(weights, axis=1, keepdims=True)
    rounded = lax.optimization_barrier(weights.astype(jnp.bfloat16)).astype(jnp.float32)
    return jnp.dot(rounded, value_head) / totals


def reference(queries, keys, values, cache_keys, cache_values, levels, first_span, level_gate):
    key_span = jnp.arange(TOKENS, dtype=jnp.int32) // CL

    def one_span(span_id):
        query_rows = lax.dynamic_slice_in_dim(queries, (span_id * CL).astype(jnp.int32), CL, 0)
        query_rows = query_rows.astype(jnp.float32).reshape(CL, HEADS, HD).transpose(1, 0, 2)
        fresh_rows = (key_span == span_id)[:, None]
        key_rows = jnp.where(fresh_rows, keys, cache_keys).astype(jnp.float32).reshape(TOKENS, HEADS, HD).transpose(1, 0, 2)
        value_rows = jnp.where(fresh_rows, values, cache_values).astype(jnp.float32).reshape(TOKENS, HEADS, HD).transpose(1, 0, 2)
        allowed = (key_span >= first_span[span_id]) & (key_span <= span_id)
        allowed_all = jnp.broadcast_to(allowed[None, :], (HEADS, TOKENS))
        mixture = lax.map(head_attend, (query_rows, key_rows, value_rows, allowed_all))
        gate_row = level_gate[levels[span_id]].reshape(HEADS, 1, HD)
        output_rows = (mixture * gate_row).transpose(1, 0, 2)
        return output_rows.reshape(CL, FEAT).astype(jnp.bfloat16)

    stacked = lax.map(one_span, jnp.arange(SPANS, dtype=jnp.int32))
    return stacked.reshape(TOKENS, FEAT)
```

```python
import functools
import math

import jax
import jax.numpy as jnp
from jax import lax
from jax.experimental import pallas as pl
from jax.experimental.pallas import tpu as pltpu
from jax.sharding import PartitionSpec as P

HD = 128
CL = 512
NX, NZ, NH = 4, 16, 8
NR = 4
J = 3
ROWS = 128
WIDTH = J * HD
TOK = 16
QS = NX * ROWS
LOW = -3.0e38
SCALE = HD**-0.5 * math.log2(math.e)
BF = jnp.bfloat16
F32 = jnp.float32
MESH = pl.DeviceIdType.MESH


def kernel(
    q_in, k_in, v_in, ck_in, cv_in, levels, first, gate_in, out,
    kb, vt, cvv, gate, q_all, k_all, v_all, qx, qt, acc, m_st, l_st,
    cq, ck2, cv2, o_send, s_send, o_cur, s_cur, p_send, ps_send, p_rec, ps_rec, o_fin,
    ring_s, ring_r, y_s, y_r, x_s, x_r, c_s, c_r, oc_s, oc_r, p_s, p_r, out_s, out_r, loc,
):
    s = lax.axis_index("span")
    h = lax.axis_index("head")
    x = s // NZ
    z = s % NZ
    zq = z // NR
    r = z % NR
    core = h % 2

    def at(xx, zz):
        return xx * NZ + zz

    right = at(x, (z + 1) % NZ)
    left = at(x, (z + NZ - 1) % NZ)

    def remote(src, dst, send, recv, span, head):
        return pltpu.make_async_remote_copy(
            src_ref=src, dst_ref=dst, send_sem=send, recv_sem=recv,
            device_id=(span, head), device_id_type=MESH,
        )

    cp_v = pltpu.make_async_copy(cv_in, cvv, loc.at[0])
    cp_k = pltpu.make_async_copy(ck_in, kb.at[0], loc.at[1])
    cp_g = pltpu.make_async_copy(gate_in, gate, loc.at[2])
    cp_v.start()
    cp_k.start()
    cp_g.start()

    barrier = pltpu.get_barrier_semaphore()
    for o in range(1, NH):
        pl.semaphore_signal(barrier, inc=1, device_id=(s, (h + o) % NH), device_id_type=MESH)
    for o in range(1, NX):
        pl.semaphore_signal(barrier, inc=1, device_id=(at((x + o) % NX, z), h), device_id_type=MESH)
    for o in range(1, NR):
        pl.semaphore_signal(
            barrier, inc=1, device_id=(at(x, zq * NR + (r + o) % NR), h), device_id_type=MESH
        )
    for n in (right, left):
        pl.semaphore_signal(barrier, inc=1, device_id=(n, h), device_id_type=MESH)

    p_rec[...] = jnp.zeros_like(p_rec)
    row8 = lax.broadcasted_iota(jnp.int32, (8, ROWS), 0)
    empty = jnp.where(row8 < J, LOW, 0.0).astype(F32)
    for i in range(NX):
        ps_rec[i] = empty
    acc[...] = jnp.zeros_like(acc)
    m_st[...] = jnp.full_like(m_st, LOW)
    l_st[...] = jnp.zeros_like(l_st)
    cp_v.wait()
    for j in range(J):
        vt[0, j * HD : (j + 1) * HD, :] = cvv[:, j * HD : (j + 1) * HD].T
    cp_k.wait()
    cp_g.wait()

    pl.semaphore_wait(barrier, NH - 1 + NX - 1 + NR - 1 + 2)

    def ring(d, kv, t):
        buf = kb if kv == 0 else vt
        if d == 0:
            return remote(buf.at[t - 1], buf.at[t], ring_s.at[d, kv, t], ring_r.at[d, kv, t], right, h)
        src = (NZ + 1 - t) % NZ if isinstance(t, int) else NZ + 1 - t
        return remote(buf.at[src], buf.at[NZ - t], ring_s.at[d, kv, t], ring_r.at[d, kv, t], left, h)

    for kv in (0, 1):
        for d in (0, 1):
            ring(d, kv, 1).start()

    fresh = ((q_in, q_all), (k_in, k_all), (v_in, v_all))

    def to_heads(i, o):
        src, dst = fresh[i]
        n = (h + o) % NH
        return remote(
            src.at[:, pl.ds(pl.multiple_of(n * WIDTH, HD), WIDTH)],
            dst.at[pl.ds(pl.multiple_of(h * TOK, TOK), TOK), :],
            y_s.at[i, o], y_r.at[i, o], s, n,
        )

    def own_heads(i):
        src, dst = fresh[i]
        return pltpu.make_async_copy(
            src.at[:, pl.ds(pl.multiple_of(h * WIDTH, HD), WIDTH)],
            dst.at[pl.ds(pl.multiple_of(h * TOK, TOK), TOK), :],
            loc.at[i],
        )

    for i in range(3):
        own_heads(i).start()
        for o in range(1, NH):
            to_heads(i, o).start()

    def heads_arrived(i):
        own_heads(i).wait()
        for o in range(1, NH):
            to_heads(i, o).wait_recv()

    def to_row(o):
        return remote(q_all, qx.at[x], x_s.at[o], x_r.at[o], at((x + o) % NX, z), h)

    heads_arrived(0)
    for o in range(1, NX):
        to_row(o).start()
    own_q = pltpu.make_async_copy(q_all, qx.at[x], loc.at[0])
    own_q.start()

    mine = r - core
    takes = (mine >= 0) & (mine < J)

    def to_taker(i, o):
        n = (r + o) % NR
        j = jnp.clip(n - core, 0, J - 1)
        src = (q_all, k_all, v_all)[i].at[:, pl.ds(pl.multiple_of(j * HD, HD), HD)]
        dst = (cq, ck2, cv2)[i].at[r]
        return remote(src, dst, c_s.at[i, o], c_r.at[i, o], at(x, zq * NR + n), h)

    def own_taken(i):
        j = jnp.clip(mine, 0, J - 1)
        src = (q_all, k_all, v_all)[i].at[:, pl.ds(pl.multiple_of(j * HD, HD), HD)]
        return pltpu.make_async_copy(src, (cq, ck2, cv2)[i].at[r], loc.at[3 + i])

    def sends_to(o):
        n = (r + o) % NR
        return (n - core >= 0) & (n - core < J)

    heads_arrived(1)
    heads_arrived(2)
    for o in range(1, NR):

        @pl.when(sends_to(o))
        def _():
            for i in range(3):
                to_taker(i, o).start()

    @pl.when(takes)
    def _():
        for i in range(3):
            own_taken(i).start()

    def forward(t):
        for kv in (0, 1):
            for d in (0, 1):
                ring(d, kv, t).wait_recv()
                ring(d, kv, t + 1).start()

    forward(1)

    own_q.wait()
    for o in range(1, NX):
        to_row(o).wait_recv()
    for i in range(NX):
        for j in range(J):
            qt[j, :, i * ROWS : (i + 1) * ROWS] = qx[i, :, j * HD : (j + 1) * HD].T

    lane_row = lax.broadcasted_iota(jnp.int32, (1, QS), 1) // ROWS
    q_span = lane_row * NR + zq
    q_first = jnp.zeros((1, QS), jnp.int32)
    for i in range(NX):
        q_first = jnp.where(lane_row == i, first[i * NR + zq], q_first)

    def sees(slot):
        c = x * NR + ((z - slot + NZ) % NZ) // NR
        return (q_first <= c) & (q_span > c)

    def attend(a, b):
        see_a, see_b = sees(a), sees(b)
        for j in range(J):
            cols = slice(j * HD, (j + 1) * HD)
            query = qt[j]
            sa = jnp.dot(kb[a, :, cols], query, preferred_element_type=F32)
            sb = jnp.dot(kb[b, :, cols], query, preferred_element_type=F32)
            ma = jnp.where(see_a, jnp.max(sa, axis=0, keepdims=True) * SCALE, LOW)
            mb = jnp.where(see_b, jnp.max(sb, axis=0, keepdims=True) * SCALE, LOW)
            old = m_st[j]
            peak = jnp.maximum(old, jnp.maximum(ma, mb))
            pa = jnp.exp2(sa * SCALE - jnp.where(see_a, peak, jnp.inf))
            pb = jnp.exp2(sb * SCALE - jnp.where(see_b, peak, jnp.inf))
            shrink = jnp.exp2(old - peak)
            m_st[j] = peak
            l_st[j] = (
                l_st[j] * shrink
                + jnp.sum(pa, axis=0, keepdims=True)
                + jnp.sum(pb, axis=0, keepdims=True)
            )
            product = jnp.dot(vt[a, cols, :], pa.astype(BF), preferred_element_type=F32)
            product += jnp.dot(vt[b, cols, :], pb.astype(BF), preferred_element_type=F32)
            acc[j] = acc[j] * shrink + product

    def step(t, carry):
        attend(t, NZ - t)
        forward(t + 1)
        return carry

    lax.fori_loop(1, 3, step, 0)

    def to_rows_of_span(i, o):
        n = (r + o) % NR
        j = jnp.clip(mine, 0, J - 1)
        src = (o_send, s_send)[i].at[n]
        dst = (o_cur, s_cur)[i].at[j]
        return remote(src, dst, oc_s.at[i, o], oc_r.at[i, o], at(x, zq * NR + n), h)

    def own_part(i):
        j = jnp.clip(mine, 0, J - 1)
        return pltpu.make_async_copy((o_send, s_send)[i].at[r], (o_cur, s_cur)[i].at[j], loc.at[3 + i])

    @pl.when(takes)
    def _():
        for i in range(3):
            own_taken(i).wait()
            for o in range(1, NR):
                to_taker(i, o).wait_recv()
        query = jnp.concatenate([cq[i].T for i in range(NR)], axis=1)
        keys = ck2[...].reshape(CL, HD)
        value = jnp.concatenate([cv2[i].T for i in range(NR)], axis=1)
        scores = jnp.dot(keys, query, preferred_element_type=F32)
        peak = jnp.max(scores, axis=0, keepdims=True) * SCALE
        weights = jnp.exp2(scores * SCALE - peak)
        total = jnp.sum(weights, axis=0, keepdims=True)
        part = jnp.dot(value, weights.astype(BF), preferred_element_type=F32) / total
        for i in range(NR):
            lanes = slice(i * ROWS, (i + 1) * ROWS)
            o_send[i] = part[:, lanes].astype(BF)
            s_send[i] = jnp.where(row8 == 0, peak[:, lanes], total[:, lanes])
        for i in range(2):
            own_part(i).start()
            for o in range(1, NR):
                to_rows_of_span(i, o).start()

    lax.fori_loop(3, 6, step, 0)

    attend(6, NZ - 6)
    for kv in (0, 1):
        for d in (0, 1):
            ring(d, kv, 7).wait_recv()
        ring(kv, kv, 8).start()
    attend(7, NZ - 7)
    for kv in (0, 1):
        ring(kv, kv, 8).wait_recv()
    attend(0, 8)

    def to_owner(i, o):
        n = (x + o) % NX
        src = (p_send, ps_send)[i].at[n]
        dst = (p_rec, ps_rec)[i].at[x]
        return remote(src, dst, p_s.at[i, o], p_r.at[i, o], at(n, z), h)

    for i in range(NX):
        lanes = slice(i * ROWS, (i + 1) * ROWS)
        stats = empty
        for j in range(J):
            total = l_st[j][:, lanes]
            p_send[i, j * HD : (j + 1) * HD, :] = (
                acc[j][:, lanes] / jnp.where(total > 0.0, total, 1.0)
            ).astype(BF)
            stats = jnp.where(row8 == j, m_st[j][:, lanes], stats)
            stats = jnp.where(row8 == J + j, total, stats)
        ps_send[i] = stats
    for o in range(1, NX):

        @pl.when(x + o < NX)
        def _():
            for i in range(2):
                to_owner(i, o).start()

    @pl.when(takes)
    def _():
        for i in range(2):
            own_part(i).wait()

    for o in range(1, NR):
        n = (r - o + NR) % NR

        @pl.when((n - core >= 0) & (n - core < J))
        def _():
            for i in range(2):
                remote(
                    (o_send, s_send)[i].at[0], (o_cur, s_cur)[i].at[jnp.clip(n - core, 0, J - 1)],
                    oc_s.at[i, o], oc_r.at[i, o], at(x, zq * NR + n), h,
                ).wait_recv()

    p_rec[x] = p_send[x]
    ps_rec[x] = ps_send[x]
    for o in range(1, NX):

        @pl.when(x - o >= 0)
        def _():
            for i in range(2):
                to_owner(i, o).wait_recv()

    level = levels[x * NR + zq]
    level_row = lax.broadcasted_iota(jnp.int32, (16, WIDTH), 0)
    gate_row = jnp.sum(jnp.where(level_row == level, gate[...], 0.0), axis=0, keepdims=True)
    for j in range(J):
        cols = slice(j * HD, (j + 1) * HD)
        stat = s_cur[j]
        peaks = [stat[0:1]] + [ps_rec[i][j : j + 1] for i in range(NX)]
        totals = [stat[1:2]] + [ps_rec[i][J + j : J + j + 1] for i in range(NX)]
        parts = [o_cur[j]] + [p_rec[i, cols, :] for i in range(NX)]
        peak = functools.reduce(jnp.maximum, peaks)
        shares = [t * jnp.exp2(p - peak) for t, p in zip(totals, peaks)]
        whole = functools.reduce(jnp.add, shares)
        mixed = functools.reduce(jnp.add, [w * p.astype(F32) for w, p in zip(shares, parts)]) / whole
        o_fin[:, cols] = (mixed.T * gate_row[:, cols]).astype(BF)

    def to_tokens(o):
        n = (h + o) % NH
        return remote(
            o_fin.at[pl.ds(pl.multiple_of(n * TOK, TOK), TOK), :],
            out.at[:, pl.ds(pl.multiple_of(h * WIDTH, HD), WIDTH)],
            out_s.at[o], out_r.at[o], s, n,
        )

    own_out = pltpu.make_async_copy(
        o_fin.at[pl.ds(pl.multiple_of(h * TOK, TOK), TOK), :],
        out.at[:, pl.ds(pl.multiple_of(h * WIDTH, HD), WIDTH)],
        loc.at[0],
    )
    for o in range(1, NH):
        to_tokens(o).start()
    own_out.start()

    for kv in (0, 1):
        for d in (0, 1):
            for t in range(1, 8):
                ring(d, kv, t).wait_send()
        ring(kv, kv, 8).wait_send()
    for i in range(3):
        for o in range(1, NH):
            to_heads(i, o).wait_send()
    for o in range(1, NX):
        to_row(o).wait_send()
    for o in range(1, NR):

        @pl.when(sends_to(o))
        def _():
            for i in range(3):
                to_taker(i, o).wait_send()

    @pl.when(takes)
    def _():
        for i in range(2):
            for o in range(1, NR):
                to_rows_of_span(i, o).wait_send()

    for o in range(1, NX):

        @pl.when(x + o < NX)
        def _():
            for i in range(2):
                to_owner(i, o).wait_send()

    own_out.wait()
    for o in range(1, NH):
        to_tokens(o).wait()


def shards(queries, keys, values, cache_keys, cache_values, levels, first_span, level_gate):
    hbm = pl.BlockSpec(memory_space=pl.ANY)
    smem = pl.BlockSpec(memory_space=pltpu.SMEM)
    dma = pltpu.SemaphoreType.DMA
    return pl.pallas_call(
        kernel,
        out_shape=jax.ShapeDtypeStruct((TOK, NH * WIDTH), BF),
        in_specs=[hbm, hbm, hbm, hbm, hbm, smem, smem, hbm],
        out_specs=hbm,
        scratch_shapes=[
            pltpu.VMEM((NZ, ROWS, WIDTH), BF),
            pltpu.VMEM((NZ, WIDTH, ROWS), BF),
            pltpu.VMEM((ROWS, WIDTH), BF),
            pltpu.VMEM((16, WIDTH), F32),
            pltpu.VMEM((ROWS, WIDTH), BF),
            pltpu.VMEM((ROWS, WIDTH), BF),
            pltpu.VMEM((ROWS, WIDTH), BF),
            pltpu.VMEM((NX, ROWS, WIDTH), BF),
            pltpu.VMEM((J, HD, QS), BF),
            pltpu.VMEM((J, HD, QS), F32),
            pltpu.VMEM((J, 1, QS), F32),
            pltpu.VMEM((J, 1, QS), F32),
            pltpu.VMEM((NR, ROWS, HD), BF),
            pltpu.VMEM((NR, ROWS, HD), BF),
            pltpu.VMEM((NR, ROWS, HD), BF),
            pltpu.VMEM((NR, HD, ROWS), BF),
            pltpu.VMEM((NR, 8, ROWS), F32),
            pltpu.VMEM((J, HD, ROWS), BF),
            pltpu.VMEM((J, 8, ROWS), F32),
            pltpu.VMEM((NX, WIDTH, ROWS), BF),
            pltpu.VMEM((NX, 8, ROWS), F32),
            pltpu.VMEM((NX, WIDTH, ROWS), BF),
            pltpu.VMEM((NX, 8, ROWS), F32),
            pltpu.VMEM((ROWS, WIDTH), BF),
            dma((2, 2, 9)),
            dma((2, 2, 9)),
            dma((3, NH)),
            dma((3, NH)),
            dma((NX,)),
            dma((NX,)),
            dma((3, NR)),
            dma((3, NR)),
            dma((2, NR)),
            dma((2, NR)),
            dma((2, NX)),
            dma((2, NX)),
            dma((NH,)),
            dma((NH,)),
            dma((6,)),
        ],
        compiler_params=pltpu.CompilerParams(
            collective_id=0, has_side_effects=True, vmem_limit_bytes=48 << 20
        ),
    )(queries, keys, values, cache_keys, cache_values, levels, first_span, level_gate)


def solution(mesh):
    tokens = P(("span", "head"), None)
    placed = (
        tokens, tokens, tokens, P("span", "head"), P("span", "head"), P(), P(), P(None, "head"),
    )
    return jax.shard_map(shards, mesh=mesh, in_specs=placed, out_specs=tokens, check_vma=False)
```

```python
import functools
import math

import jax
import jax.numpy as jnp
from jax import lax
from jax.experimental import pallas as pl
from jax.experimental.pallas import tpu as pltpu
from jax.sharding import PartitionSpec as P

HD = 128
CL = 512
NX, NZ, NH = 4, 16, 8
NR = 4
J = 3
ROWS = 128
WIDTH = J * HD
TOK = 16
QS = NX * ROWS
LOW = -3.0e38
SCALE = HD**-0.5 * math.log2(math.e)
BF = jnp.bfloat16
F32 = jnp.float32
MESH = pl.DeviceIdType.MESH


def kernel(
    q_in, k_in, v_in, ck_in, cv_in, levels_in, first_in, gate_in, out,
    levels, first, kb, vt, cvv, gate, q_all, k_all, v_all, qx, qt, acc, m_st, l_st,
    cq, ck2, cv2, o_send, o_cur, p_send, p_rec, o_fin,
    ring_s, ring_r, y_s, y_r, x_s, x_r, c_s, c_r, oc_s, oc_r, p_s, p_r, out_s, out_r, loc, fetch,
):
    s = lax.axis_index("span")
    h = lax.axis_index("head")
    x = s // NZ
    z = s % NZ
    zq = z // NR
    r = z % NR
    core = h % 2

    def at(xx, zz):
        return xx * NZ + zz

    right = at(x, (z + 1) % NZ)
    left = at(x, (z + NZ - 1) % NZ)

    def remote(src, dst, send, recv, span, head):
        return pltpu.make_async_remote_copy(
            src_ref=src, dst_ref=dst, send_sem=send, recv_sem=recv,
            device_id=(span, head), device_id_type=MESH,
        )

    barrier = pltpu.get_barrier_semaphore()
    for n in (right, left):
        pl.semaphore_signal(barrier, inc=1, device_id=(n, h), device_id_type=MESH)
    for o in range(1, NR):
        pl.semaphore_signal(
            barrier, inc=1, device_id=(at(x, zq * NR + (r + o) % NR), h), device_id_type=MESH
        )
    for o in range(1, NX):
        pl.semaphore_signal(barrier, inc=1, device_id=(at((x + o) % NX, z), h), device_id_type=MESH)
    for o in range(1, NH):
        pl.semaphore_signal(barrier, inc=1, device_id=(s, (h + o) % NH), device_id_type=MESH)

    operands = (
        (cv_in, cvv), (ck_in, kb.at[0]), (gate_in, gate), (levels_in, levels), (first_in, first),
    )
    fetched = [pltpu.make_async_copy(a, b, fetch.at[i]) for i, (a, b) in enumerate(operands)]
    for copy in fetched:
        copy.start()
    fetched[0].wait()
    for j in range(J):
        vt[0, j * HD : (j + 1) * HD, :] = cvv[:, j * HD : (j + 1) * HD].T
    fetched[1].wait()

    pl.semaphore_wait(barrier, 2 + NR - 1 + NX - 1 + NH - 1)

    def ring(d, kv, c, t):
        buf, half = ((kb, ROWS // 2), (vt, WIDTH // 2))[kv]
        rows = pl.ds(c * half, half)
        if d == 0:
            src, dst, n = t - 1, t, right
        else:
            src, dst, n = (NZ + 1 - t if not isinstance(t, int) or t > 1 else 0), NZ - t, left
        return remote(
            buf.at[src, rows], buf.at[dst, rows], ring_s.at[d, kv, c, t], ring_r.at[d, kv, c, t], n, h
        )

    halves = [(kv, c) for kv in (0, 1) for c in (0, 1)]
    for kv, c in halves:
        for d in (0, 1):
            ring(d, kv, c, 1).start()

    fresh = ((q_in, q_all), (k_in, k_all), (v_in, v_all))

    def to_heads(i, o):
        src, dst = fresh[i]
        n = (h + o) % NH
        return remote(
            src.at[:, pl.ds(pl.multiple_of(n * WIDTH, HD), WIDTH)],
            dst.at[pl.ds(pl.multiple_of(h * TOK, TOK), TOK), :],
            y_s.at[i, o], y_r.at[i, o], s, n,
        )

    def own_heads(i):
        src, dst = fresh[i]
        return pltpu.make_async_copy(
            src.at[:, pl.ds(pl.multiple_of(h * WIDTH, HD), WIDTH)],
            dst.at[pl.ds(pl.multiple_of(h * TOK, TOK), TOK), :],
            loc.at[i],
        )

    for i in range(3):
        own_heads(i).start()
        for o in range(1, NH):
            to_heads(i, o).start()

    def heads_arrived(i):
        own_heads(i).wait()
        for o in range(1, NH):
            to_heads(i, o).wait_recv()

    def to_row(o):
        return remote(q_all, qx.at[x], x_s.at[o], x_r.at[o], at((x + o) % NX, z), h)

    mine = r - core
    takes = (mine >= 0) & (mine < J)

    def to_taker(i, o):
        n = (r + o) % NR
        j = jnp.clip(n - core, 0, J - 1)
        src = (q_all, k_all, v_all)[i].at[:, pl.ds(pl.multiple_of(j * HD, HD), HD)]
        dst = (cq, ck2, cv2)[i].at[r]
        return remote(src, dst, c_s.at[i, o], c_r.at[i, o], at(x, zq * NR + n), h)

    def own_taken(i):
        j = jnp.clip(mine, 0, J - 1)
        src = (q_all, k_all, v_all)[i].at[:, pl.ds(pl.multiple_of(j * HD, HD), HD)]
        return pltpu.make_async_copy(src, (cq, ck2, cv2)[i].at[r], loc.at[3 + i])

    def sends_to(o):
        n = (r + o) % NR
        return (n - core >= 0) & (n - core < J)

    def forward(t):
        for kv, c in halves:
            for d in (0, 1):
                ring(d, kv, c, t).wait_recv()
                ring(d, kv, c, t + 1).start()

    forward(1)

    heads_arrived(0)
    for o in range(1, NX):
        to_row(o).start()
    own_q = pltpu.make_async_copy(q_all, qx.at[x], loc.at[0])
    own_q.start()

    heads_arrived(1)
    heads_arrived(2)
    for o in range(1, NR):

        @pl.when(sends_to(o))
        def _():
            for i in range(3):
                to_taker(i, o).start()

    @pl.when(takes)
    def _():
        for i in range(3):
            own_taken(i).start()

    forward(2)

    acc[...] = jnp.zeros_like(acc)
    m_st[...] = jnp.full_like(m_st, LOW)
    l_st[...] = jnp.zeros_like(l_st)
    for i in range(1, NX):

        @pl.when(i > x)
        def _():
            p_rec[i] = jnp.zeros((J, HD + 16, ROWS), BF)

    for i in range(2, 5):
        fetched[i].wait()
    own_q.wait()
    for o in range(1, NX):
        to_row(o).wait_recv()
    for i in range(NX):
        for j in range(J):
            qt[j, :, i * ROWS : (i + 1) * ROWS] = qx[i, :, j * HD : (j + 1) * HD].T

    lane_row = lax.broadcasted_iota(jnp.int32, (1, QS), 1) // ROWS
    q_span = lane_row * NR + zq
    q_first = jnp.zeros((1, QS), jnp.int32)
    for i in range(NX):
        q_first = jnp.where(lane_row == i, first[i * NR + zq], q_first)

    def sees(slot):
        c = x * NR + ((z - slot + NZ) % NZ) // NR
        return (q_first <= c) & (q_span > c)

    def attend_head(j, slots):
        cols = slice(j * HD, (j + 1) * HD)
        query = qt[j]
        seen = [sees(i) for i in slots]
        scores = [jnp.dot(kb[i, :, cols], query, preferred_element_type=F32) for i in slots]
        old = m_st[j]
        peak = old
        for see, score in zip(seen, scores):
            peak = jnp.maximum(peak, jnp.where(see, jnp.max(score, axis=0, keepdims=True) * SCALE, LOW))
        shrink = jnp.exp2(old - peak)
        total = l_st[j] * shrink
        product = acc[j] * shrink
        for i, see, score in zip(slots, seen, scores):
            weight = jnp.exp2(score * SCALE - jnp.where(see, peak, jnp.inf))
            total += jnp.sum(weight, axis=0, keepdims=True)
            product += jnp.dot(vt[i, cols, :], weight.astype(BF), preferred_element_type=F32)
        m_st[j] = peak
        l_st[j] = total
        acc[j] = product

    def attend(*slots):
        for j in range(J):
            attend_head(j, slots)

    def packed(part, peak, total):
        row = lax.broadcasted_iota(jnp.int32, (16, ROWS), 0)
        tile = jnp.zeros((16, ROWS), F32)
        for first_row, value in ((0, peak), (3, total)):
            for i in range(3):
                piece = value.astype(BF).astype(F32)
                tile = jnp.where(row == first_row + i, piece, tile)
                value = value - piece
        return jnp.concatenate([part, tile], axis=0).astype(BF)

    def unpacked(block):
        tile = block[HD:].astype(F32)
        return block[:HD].astype(F32), tile[0:1] + tile[1:2] + tile[2:3], tile[3:4] + tile[4:5] + tile[5:6]

    attend(0)
    attend(1, NZ - 1)
    forward(3)
    attend(2, NZ - 2)
    forward(4)

    def to_rows_of_span(o):
        n = (r + o) % NR
        j = jnp.clip(mine, 0, J - 1)
        return remote(o_send.at[n], o_cur.at[j], oc_s.at[o], oc_r.at[o], at(x, zq * NR + n), h)

    own_part = pltpu.make_async_copy(o_send.at[r], o_cur.at[jnp.clip(mine, 0, J - 1)], loc.at[3])

    @pl.when(takes)
    def _():
        for i in range(3):
            own_taken(i).wait()
            for o in range(1, NR):
                to_taker(i, o).wait_recv()
        query = jnp.concatenate([cq[i].T for i in range(NR)], axis=1)
        keys = ck2[...].reshape(CL, HD)
        value = jnp.concatenate([cv2[i].T for i in range(NR)], axis=1)
        scores = jnp.dot(keys, query, preferred_element_type=F32)
        peak = jnp.max(scores, axis=0, keepdims=True) * SCALE
        weights = jnp.exp2(scores * SCALE - peak)
        total = jnp.sum(weights, axis=0, keepdims=True)
        part = jnp.dot(value, weights.astype(BF), preferred_element_type=F32) / total
        for i in range(NR):
            lanes = slice(i * ROWS, (i + 1) * ROWS)
            o_send[i] = packed(part[:, lanes], peak[:, lanes], total[:, lanes])
        own_part.start()
        for o in range(1, NR):
            to_rows_of_span(o).start()

    forward(5)
    attend(3, NZ - 3)
    attend(4, NZ - 4)
    forward(6)
    attend(5, NZ - 5)
    for kv, c in halves:
        for d in (0, 1):
            ring(d, kv, c, 7).wait_recv()
        ring(kv, kv, c, 8).start()
    attend(6, NZ - 6)
    attend(7, NZ - 7)

    level = levels[x * NR + zq]
    level_row = lax.broadcasted_iota(jnp.int32, (16, WIDTH), 0)
    gate_row = jnp.sum(jnp.where(level_row == level, gate[...], 0.0), axis=0, keepdims=True)

    def to_owner(j, o):
        n = (x + o) % NX
        return remote(p_send.at[n, j], p_rec.at[x, j], p_s.at[j, o], p_r.at[j, o], at(n, z), h)

    for kv, c in halves:
        ring(kv, kv, c, 8).wait_recv()
    for j in range(J):
        attend_head(j, (8,))
        for i in range(NX):
            lanes = slice(i * ROWS, (i + 1) * ROWS)
            total = l_st[j][:, lanes]
            part = acc[j][:, lanes] / jnp.where(total > 0.0, total, 1.0)
            p_send[i, j] = packed(part, m_st[j][:, lanes], total)
        for o in range(1, NX):

            @pl.when(x + o < NX)
            def _():
                to_owner(j, o).start()

    for kv, c in halves:
        for d in (0, 1):
            for t in range(1, 8):
                ring(d, kv, c, t).wait_send()
        ring(kv, kv, c, 8).wait_send()
    for i in range(3):
        for o in range(1, NH):
            to_heads(i, o).wait_send()
    for o in range(1, NX):
        to_row(o).wait_send()
    for o in range(1, NR):

        @pl.when(sends_to(o))
        def _():
            for i in range(3):
                to_taker(i, o).wait_send()

    @pl.when(takes)
    def _():
        own_part.wait()
        for o in range(1, NR):
            to_rows_of_span(o).wait_send()

    for o in range(1, NR):
        n = (r - o + NR) % NR

        @pl.when((n - core >= 0) & (n - core < J))
        def _():
            remote(
                o_send.at[0], o_cur.at[jnp.clip(n - core, 0, J - 1)], oc_s.at[o], oc_r.at[o],
                at(x, zq * NR + n), h,
            ).wait_recv()

    def to_tokens(j, o):
        n = (h + o) % NH
        return remote(
            o_fin.at[j, pl.ds(pl.multiple_of(n * TOK, TOK), TOK), :],
            out.at[:, pl.ds(pl.multiple_of(h * WIDTH + j * HD, HD), HD)],
            out_s.at[j, o], out_r.at[j, o], s, n,
        )

    def own_tokens(j):
        return pltpu.make_async_copy(
            o_fin.at[j, pl.ds(pl.multiple_of(h * TOK, TOK), TOK), :],
            out.at[:, pl.ds(pl.multiple_of(h * WIDTH + j * HD, HD), HD)],
            loc.at[j],
        )

    for j in range(J):
        for o in range(1, NX):

            @pl.when(x - o >= 0)
            def _():
                to_owner(j, o).wait_recv()

        p_rec[x, j] = p_send[x, j]
        parts = [unpacked(o_cur[j])]
        for i in range(NX):
            part, peak, total = unpacked(p_rec[i, j])
            parts.append((part, jnp.where(i <= x, peak, LOW), jnp.where(i <= x, total, 0.0)))
        peak = functools.reduce(jnp.maximum, [p for _, p, _ in parts])
        shares = [t * jnp.exp2(p - peak) for _, p, t in parts]
        whole = functools.reduce(jnp.add, shares)
        mixed = functools.reduce(jnp.add, [w * p for w, (p, _, _) in zip(shares, parts)]) / whole
        o_fin[j] = (mixed.T * gate_row[:, j * HD : (j + 1) * HD]).astype(BF)
        for o in range(1, NH):
            to_tokens(j, o).start()
        own_tokens(j).start()

    for j in range(J):
        for o in range(1, NX):

            @pl.when(x + o < NX)
            def _():
                to_owner(j, o).wait_send()

        own_tokens(j).wait()
        for o in range(1, NH):
            to_tokens(j, o).wait()


def shards(queries, keys, values, cache_keys, cache_values, levels, first_span, level_gate):
    hbm = pl.BlockSpec(memory_space=pltpu.HBM)
    dma = pltpu.SemaphoreType.DMA
    return pl.pallas_call(
        kernel,
        out_shape=pltpu.VMEM((TOK, NH * WIDTH), BF),
        in_specs=[hbm] * 8,
        out_specs=pl.BlockSpec(memory_space=pltpu.VMEM),
        scratch_shapes=[
            pltpu.SMEM((16,), jnp.int32),
            pltpu.SMEM((16,), jnp.int32),
            pltpu.VMEM((NZ, ROWS, WIDTH), BF),
            pltpu.VMEM((NZ, WIDTH, ROWS), BF),
            pltpu.VMEM((ROWS, WIDTH), BF),
            pltpu.VMEM((16, WIDTH), F32),
            pltpu.VMEM((ROWS, WIDTH), BF),
            pltpu.VMEM((ROWS, WIDTH), BF),
            pltpu.VMEM((ROWS, WIDTH), BF),
            pltpu.VMEM((NX, ROWS, WIDTH), BF),
            pltpu.VMEM((J, HD, QS), BF),
            pltpu.VMEM((J, HD, QS), F32),
            pltpu.VMEM((J, 1, QS), F32),
            pltpu.VMEM((J, 1, QS), F32),
            pltpu.VMEM((NR, ROWS, HD), BF),
            pltpu.VMEM((NR, ROWS, HD), BF),
            pltpu.VMEM((NR, ROWS, HD), BF),
            pltpu.VMEM((NR, HD + 16, ROWS), BF),
            pltpu.VMEM((J, HD + 16, ROWS), BF),
            pltpu.VMEM((NX, J, HD + 16, ROWS), BF),
            pltpu.VMEM((NX, J, HD + 16, ROWS), BF),
            pltpu.VMEM((J, ROWS, HD), BF),
            dma((2, 2, 2, 9)),
            dma((2, 2, 2, 9)),
            dma((3, NH)),
            dma((3, NH)),
            dma((NX,)),
            dma((NX,)),
            dma((3, NR)),
            dma((3, NR)),
            dma((NR,)),
            dma((NR,)),
            dma((J, NX)),
            dma((J, NX)),
            dma((J, NH)),
            dma((J, NH)),
            dma((6,)),
            dma((5,)),
        ],
        compiler_params=pltpu.CompilerParams(
            collective_id=0, has_side_effects=True, vmem_limit_bytes=63 << 20
        ),
    )(queries, keys, values, cache_keys, cache_values, levels, first_span, level_gate)


def solution(mesh):
    tokens = P(("span", "head"), None)
    placed = (
        tokens, tokens, tokens, P("span", "head"), P("span", "head"), P(), P(), P(None, "head"),
    )
    return jax.shard_map(shards, mesh=mesh, in_specs=placed, out_specs=tokens, check_vma=False)
```

```python
import functools
import math

import jax
import jax.numpy as jnp
from jax import lax
from jax.experimental import pallas as pl
from jax.experimental.pallas import tpu as pltpu
from jax.sharding import PartitionSpec as P

HD = 128
CL = 512
NX, NZ, NH = 4, 16, 8
NR = 4
J = 3
ROWS = 128
WIDTH = J * HD
TOK = 16
QS = NX * ROWS
LOW = -3.0e38
SCALE = HD**-0.5 * math.log2(math.e)
BF = jnp.bfloat16
F32 = jnp.float32
MESH = pl.DeviceIdType.MESH


def kernel(
    q_in, k_in, v_in, ck_in, cv_in, levels_in, first_in, gate_in, out,
    levels, first, kb, vt, cvv, gate, q_all, k_all, v_all, qx, qt, acc, m_st, l_st,
    cq, ck2, cv2, o_send, o_cur, p_send, p_rec, gate_cols,
    ring_s, ring_r, y_s, y_r, x_s, x_r, c_s, c_r, oc_s, oc_r, p_s, p_r, loc, fetch,
):
    s = lax.axis_index("span")
    h = lax.axis_index("head")
    x = s // NZ
    z = s % NZ
    zq = z // NR
    r = z % NR
    core = h % 2

    def at(xx, zz):
        return xx * NZ + zz

    right = at(x, (z + 1) % NZ)
    left = at(x, (z + NZ - 1) % NZ)

    def remote(src, dst, send, recv, span, head):
        return pltpu.make_async_remote_copy(
            src_ref=src, dst_ref=dst, send_sem=send, recv_sem=recv,
            device_id=(span, head), device_id_type=MESH,
        )

    barrier = pltpu.get_barrier_semaphore()
    for n in (right, left):
        pl.semaphore_signal(barrier, inc=1, device_id=(n, h), device_id_type=MESH)
    for o in range(1, NR):
        pl.semaphore_signal(
            barrier, inc=1, device_id=(at(x, zq * NR + (r + o) % NR), h), device_id_type=MESH
        )
    for o in range(1, NX):
        pl.semaphore_signal(barrier, inc=1, device_id=(at((x + o) % NX, z), h), device_id_type=MESH)
    for o in range(1, NH):
        pl.semaphore_signal(barrier, inc=1, device_id=(s, (h + o) % NH), device_id_type=MESH)

    operands = (
        (cv_in, cvv), (ck_in, kb.at[0]), (gate_in, gate), (levels_in, levels), (first_in, first),
    )
    fetched = [pltpu.make_async_copy(a, b, fetch.at[i]) for i, (a, b) in enumerate(operands)]
    for copy in fetched:
        copy.start()
    pl.semaphore_wait(barrier, 2 + NR - 1 + NX - 1 + NH - 1)

    def ring(d, kv, c, t):
        buf, half = ((kb, ROWS // 2), (vt, WIDTH // 2))[kv]
        rows = pl.ds(c * half, half)
        if d == 0:
            src, dst, n = t - 1, t, right
        else:
            src, dst, n = (NZ + 1 - t) % NZ, NZ - t, left
        source = ck_in.at[rows] if t == 1 and kv == 0 else buf.at[src, rows]
        return remote(source, buf.at[dst, rows], ring_s.at[d, kv, c, t], ring_r.at[d, kv, c, t], n, h)

    halves = [(kv, c) for kv in (0, 1) for c in (0, 1)]
    fresh = ((q_in, q_all), (k_in, k_all), (v_in, v_all))

    def to_heads(i, o):
        src, dst = fresh[i]
        n = (h + o) % NH
        return remote(
            src.at[:, pl.ds(pl.multiple_of(n * WIDTH, HD), WIDTH)],
            dst.at[pl.ds(pl.multiple_of(h * TOK, TOK), TOK), :],
            y_s.at[i, o], y_r.at[i, o], s, n,
        )

    def own_heads(i):
        src, dst = fresh[i]
        return pltpu.make_async_copy(
            src.at[:, pl.ds(pl.multiple_of(h * WIDTH, HD), WIDTH)],
            dst.at[pl.ds(pl.multiple_of(h * TOK, TOK), TOK), :],
            loc.at[i],
        )

    def send_heads(i):
        own_heads(i).start()
        for o in range(1, NH):
            to_heads(i, o).start()

    send_heads(0)
    for c in (0, 1):
        for d in (0, 1):
            ring(d, 0, c, 1).start()
    fetched[0].wait()
    for j in range(J):
        vt[0, j * HD : (j + 1) * HD, :] = cvv[:, j * HD : (j + 1) * HD].T
    for c in (0, 1):
        for d in (0, 1):
            ring(d, 1, c, 1).start()
    send_heads(1)
    send_heads(2)

    def heads_arrived(i):
        own_heads(i).wait()
        for o in range(1, NH):
            to_heads(i, o).wait_recv()

    def to_row(o):
        return remote(q_all, qx.at[x], x_s.at[o], x_r.at[o], at((x + o) % NX, z), h)

    mine = r - core
    takes = (mine >= 0) & (mine < J)

    def to_taker(i, o):
        n = (r + o) % NR
        j = jnp.clip(n - core, 0, J - 1)
        src = (q_all, k_all, v_all)[i].at[:, pl.ds(pl.multiple_of(j * HD, HD), HD)]
        dst = (cq, ck2, cv2)[i].at[r]
        return remote(src, dst, c_s.at[i, o], c_r.at[i, o], at(x, zq * NR + n), h)

    def own_taken(i):
        j = jnp.clip(mine, 0, J - 1)
        src = (q_all, k_all, v_all)[i].at[:, pl.ds(pl.multiple_of(j * HD, HD), HD)]
        return pltpu.make_async_copy(src, (cq, ck2, cv2)[i].at[r], loc.at[3 + i])

    def sends_to(o):
        n = (r + o) % NR
        return (n - core >= 0) & (n - core < J)

    def forward(t, *work):
        for n, (kv, c) in enumerate(halves):
            for d in (0, 1):
                ring(d, kv, c, t).wait_recv()
                if t < 7:
                    ring(d, kv, c, t + 1).start()
            if t == 7:
                last(kv, c, "start")
            for item in work[n : n + 1]:
                item()

    def sent(t):
        for kv, c in halves:
            for d in (0, 1):
                ring(d, kv, c, t).wait_send()

    def last(kv, c, what):
        getattr(ring(kv, kv, c, 8), what)()

    own_q = pltpu.make_async_copy(q_all, qx.at[x], loc.at[0])

    def share_queries():
        heads_arrived(0)
        for o in range(1, NX):
            to_row(o).start()
        own_q.start()

    def share_current():
        heads_arrived(2)
        for o in range(1, NR):

            @pl.when(sends_to(o))
            def _():
                for i in range(3):
                    to_taker(i, o).start()

        @pl.when(takes)
        def _():
            for i in range(3):
                own_taken(i).start()

    def clear():
        acc[...] = jnp.zeros_like(acc)
        m_st[...] = jnp.full_like(m_st, LOW)
        l_st[...] = jnp.zeros_like(l_st)
        for i in range(1, NX):

            @pl.when(i > x)
            def _():
                p_rec[i] = jnp.zeros((NH, TOK, WIDTH + HD), BF)

    forward(1)
    share_queries()
    heads_arrived(1)
    share_current()
    clear()

    def spread_gate(i):
        if i == 0:
            for n in range(2, 5):
                fetched[n].wait()
        level_row = lax.broadcasted_iota(jnp.int32, (16, WIDTH), 0)
        gate_row = jnp.sum(
            jnp.where(level_row == levels[i * NR + zq], gate[...], 0.0), axis=0, keepdims=True
        )
        for j in range(J):
            gate_cols[i, j] = jnp.broadcast_to(gate_row[:, j * HD : (j + 1) * HD], (ROWS, HD)).T

    forward(2, *[functools.partial(spread_gate, i) for i in range(NX)])

    fetched[1].wait()

    def turn_queries(j):
        if j == 0:
            own_q.wait()
            for o in range(1, NX):
                to_row(o).wait_recv()
        for i in range(NX):
            qt[j, :, i * ROWS : (i + 1) * ROWS] = qx[i, :, j * HD : (j + 1) * HD].T

    forward(3, *[functools.partial(turn_queries, j) for j in range(J)])

    lane_row = lax.broadcasted_iota(jnp.int32, (1, QS), 1) // ROWS
    q_span = lane_row * NR + zq
    q_first = jnp.zeros((1, QS), jnp.int32)
    for i in range(NX):
        q_first = jnp.where(lane_row == i, first[i * NR + zq], q_first)

    def sees(slot):
        c = x * NR + ((z - slot + NZ) % NZ) // NR
        return (q_first <= c) & (q_span > c)

    def attend_head(j, slots):
        cols = slice(j * HD, (j + 1) * HD)
        query = qt[j]
        seen = [sees(i) for i in slots]
        scores = [jnp.dot(kb[i, :, cols], query, preferred_element_type=F32) for i in slots]
        old = m_st[j]
        peak = old
        for see, score in zip(seen, scores):
            peak = jnp.maximum(peak, jnp.where(see, jnp.max(score, axis=0, keepdims=True) * SCALE, LOW))
        shrink = jnp.exp2(old - peak)
        total = l_st[j] * shrink
        product = acc[j] * shrink
        for i, see, score in zip(slots, seen, scores):
            weight = jnp.exp2(score * SCALE - jnp.where(see, peak, jnp.inf))
            total += jnp.sum(weight, axis=0, keepdims=True)
            product += jnp.dot(vt[i, cols, :], weight.astype(BF), preferred_element_type=F32)
        m_st[j] = peak
        l_st[j] = total
        acc[j] = product

    def head(j, *slots):
        return functools.partial(attend_head, j, slots)

    def both(*items):
        def run():
            for item in items:
                item()

        return run

    def packed(part, peak, total):
        row = lax.broadcasted_iota(jnp.int32, (16, ROWS), 0)
        tile = jnp.zeros((16, ROWS), F32)
        for first_row, value in ((0, peak), (3, total)):
            for i in range(3):
                piece = value.astype(BF).astype(F32)
                tile = jnp.where(row == first_row + i, piece, tile)
                value = value - piece
        return jnp.concatenate([part, tile], axis=0).astype(BF)

    def unpacked(block):
        tile = block[HD:].astype(F32)
        return block[:HD].astype(F32), tile[0:1] + tile[1:2] + tile[2:3], tile[3:4] + tile[4:5] + tile[5:6]

    def to_rows_of_span(o):
        n = (r + o) % NR
        j = jnp.clip(mine, 0, J - 1)
        return remote(o_send.at[n], o_cur.at[j], oc_s.at[o], oc_r.at[o], at(x, zq * NR + n), h)

    own_part = pltpu.make_async_copy(o_send.at[r], o_cur.at[jnp.clip(mine, 0, J - 1)], loc.at[3])

    def current(n):
        @pl.when(takes)
        def _():
            if n == 0:
                for i in range(3):
                    own_taken(i).wait()
                    for o in range(1, NR):
                        to_taker(i, o).wait_recv()
            keys = ck2[...].reshape(CL, HD)
            scores = jnp.dot(keys, cq[n].T, preferred_element_type=F32)
            peak = jnp.max(scores, axis=0, keepdims=True) * SCALE
            weights = jnp.exp2(scores * SCALE - peak)
            total = jnp.sum(weights, axis=0, keepdims=True)
            value = jnp.concatenate([cv2[i].T for i in range(NR)], axis=1)
            part = jnp.dot(value, weights.astype(BF), preferred_element_type=F32) * (1.0 / total)
            o_send[n] = packed(part, peak, total)
            if n == NR - 1:
                own_part.start()
                for o in range(1, NR):
                    to_rows_of_span(o).start()

    def current_arrived():
        @pl.when(takes)
        def _():
            own_part.wait()

        for o in range(1, NR):
            n = (r - o + NR) % NR

            @pl.when((n - core >= 0) & (n - core < J))
            def _():
                remote(
                    o_send.at[0], o_cur.at[jnp.clip(n - core, 0, J - 1)], oc_s.at[o], oc_r.at[o],
                    at(x, zq * NR + n), h,
                ).wait_recv()

    def merge_current(j):
        part, peak, total = unpacked(o_cur[j])
        lanes = pl.ds(pl.multiple_of(x * ROWS, ROWS), ROWS)
        old = m_st[j, :, lanes]
        new = jnp.maximum(old, peak)
        shrink, share = jnp.exp2(old - new), total * jnp.exp2(peak - new)
        m_st[j, :, lanes] = new
        l_st[j, :, lanes] = l_st[j, :, lanes] * shrink + share
        acc[j, :, lanes] = acc[j, :, lanes] * shrink + part * share

    def sent_entry():
        for i in range(3):
            for o in range(1, NH):
                to_heads(i, o).wait_send()
        for o in range(1, NX):
            to_row(o).wait_send()

    def sent_current():
        for o in range(1, NR):

            @pl.when(sends_to(o))
            def _():
                for i in range(3):
                    to_taker(i, o).wait_send()

        @pl.when(takes)
        def _():
            for o in range(1, NR):
                to_rows_of_span(o).wait_send()

    cur = [functools.partial(current, n) for n in range(NR)]
    merge = [functools.partial(merge_current, j) for j in range(J)]
    sent(1)
    forward(4, head(0, 0, 1, 15), head(1, 0, 1, 15), head(2, 0, 1, 15), cur[0])
    sent(2)
    forward(5, cur[1], cur[2], cur[3], both(head(0, 2, 14), sent_entry))
    sent(3)
    forward(
        6,
        both(head(1, 2, 14), head(2, 2, 14)), both(head(0, 3, 13), head(1, 3, 13)),
        both(head(2, 3, 13), head(0, 4, 12)), both(head(1, 4, 12), head(2, 4, 12)),
    )
    sent(4)
    forward(
        7,
        both(head(0, 5, 11), head(1, 5, 11)), both(head(2, 5, 11), current_arrived, sent_current),
        both(head(0, 6, 10), head(1, 6, 10)), both(head(2, 6, 10), *merge),
    )
    for j in range(J):
        attend_head(j, (7, 9))
    sent(5)
    sent(6)

    def to_owner(i, n):
        return remote(
            p_send.at[i, pl.ds(pl.multiple_of(n * TOK, TOK), TOK), :], p_rec.at[x, h],
            p_s.at[i, n], p_r.at[x, h], at(i, z), n,
        )

    def from_part(i, n):
        return remote(p_send.at[i, pl.ds(0, TOK), :], p_rec.at[i, n], p_s.at[i, n], p_r.at[i, n], at(i, z), n)

    own_tokens = pltpu.make_async_copy(
        p_send.at[x, pl.ds(pl.multiple_of(h * TOK, TOK), TOK), :], p_rec.at[x, h], loc.at[0]
    )

    def logs(i):
        lanes = slice(i * ROWS, (i + 1) * ROWS)
        row = lax.broadcasted_iota(jnp.int32, (ROWS, ROWS), 0)
        tile = jnp.zeros((ROWS, ROWS), F32)
        for j in range(J):
            total = l_st[j][:, lanes]
            value = jnp.where(
                total > 0.0,
                m_st[j][:, lanes] + jnp.log(jnp.where(total > 0.0, total, 1.0)) * math.log2(math.e),
                LOW,
            )
            for n in range(3):
                piece = value.astype(BF).astype(F32)
                tile = jnp.where(row == 3 * n + j, piece, tile)
                value = value - piece
        return tile.T

    for kv, c in halves:
        last(kv, c, "wait_recv")
    for j in range(J):
        attend_head(j, (8,))
    for i in reversed(range(NX)):

        @pl.when(i >= x)
        def _():
            lanes = slice(i * ROWS, (i + 1) * ROWS)
            for j in range(J):
                total = l_st[j][:, lanes]
                part = acc[j][:, lanes] * (1.0 / jnp.where(total > 0.0, total, 1.0)) * gate_cols[i, j]
                p_send[i, :, j * HD : (j + 1) * HD] = part.astype(BF).T
            p_send[i, :, WIDTH:] = logs(i).astype(BF)
            for o in range(1, NH):
                to_owner(i, (h + o) % NH).start()

            @pl.when(i > x)
            def _():
                to_owner(i, h).start()

            @pl.when(i == x)
            def _():
                own_tokens.start()

    sent(7)
    for kv, c in halves:
        last(kv, c, "wait_send")
    own_tokens.wait()
    for n in range(NH):
        for i in range(NX):

            @pl.when((i < x) | ((i == x) & (n != h)))
            def _():
                from_part(i, n).wait_recv()

        marks = []
        for i in range(NX):
            tile = p_rec[i, n, :, WIDTH:].astype(F32)
            mark = tile + pltpu.roll(tile, ROWS - 3, 1) + pltpu.roll(tile, ROWS - 6, 1)
            marks.append(jnp.where(i <= x, mark, LOW))
        peak = functools.reduce(jnp.maximum, marks)
        shares = [jnp.exp2(m - peak) for m in marks]
        scale = 1.0 / functools.reduce(jnp.add, shares)
        shares = [w * scale for w in shares]
        for j in range(J):
            cols = slice(j * HD, (j + 1) * HD)
            mixed = functools.reduce(
                jnp.add, [w[:, j : j + 1] * p_rec[i, n, :, cols].astype(F32) for i, w in enumerate(shares)]
            )
            out[:, n * WIDTH + j * HD : n * WIDTH + (j + 1) * HD] = mixed.astype(BF)

    for i in range(NX):
        for n in range(NH):

            @pl.when((i > x) | ((i == x) & (n != h)))
            def _():
                to_owner(i, n).wait_send()


def shards(queries, keys, values, cache_keys, cache_values, levels, first_span, level_gate):
    hbm = pl.BlockSpec(memory_space=pltpu.HBM)
    dma = pltpu.SemaphoreType.DMA
    return pl.pallas_call(
        kernel,
        out_shape=pltpu.VMEM((TOK, NH * WIDTH), BF),
        in_specs=[hbm] * 8,
        out_specs=pl.BlockSpec(memory_space=pltpu.VMEM),
        scratch_shapes=[
            pltpu.SMEM((16,), jnp.int32),
            pltpu.SMEM((16,), jnp.int32),
            pltpu.VMEM((NZ, ROWS, WIDTH), BF),
            pltpu.VMEM((NZ, WIDTH, ROWS), BF),
            pltpu.VMEM((ROWS, WIDTH), BF),
            pltpu.VMEM((16, WIDTH), F32),
            pltpu.VMEM((ROWS, WIDTH), BF),
            pltpu.VMEM((ROWS, WIDTH), BF),
            pltpu.VMEM((ROWS, WIDTH), BF),
            pltpu.VMEM((NX, ROWS, WIDTH), BF),
            pltpu.VMEM((J, HD, QS), BF),
            pltpu.VMEM((J, HD, QS), F32),
            pltpu.VMEM((J, 1, QS), F32),
            pltpu.VMEM((J, 1, QS), F32),
            pltpu.VMEM((NR, ROWS, HD), BF),
            pltpu.VMEM((NR, ROWS, HD), BF),
            pltpu.VMEM((NR, ROWS, HD), BF),
            pltpu.VMEM((NR, HD + 16, ROWS), BF),
            pltpu.VMEM((J, HD + 16, ROWS), BF),
            pltpu.VMEM((NX, ROWS, WIDTH + HD), BF),
            pltpu.VMEM((NX, NH, TOK, WIDTH + HD), BF),
            pltpu.VMEM((NX, J, HD, ROWS), F32),
            dma((2, 2, 2, 9)),
            dma((2, 2, 2, 9)),
            dma((3, NH)),
            dma((3, NH)),
            dma((NX,)),
            dma((NX,)),
            dma((3, NR)),
            dma((3, NR)),
            dma((NR,)),
            dma((NR,)),
            dma((NX, NH)),
            dma((NX, NH)),
            dma((6,)),
            dma((5,)),
        ],
        compiler_params=pltpu.CompilerParams(
            collective_id=0, has_side_effects=True, vmem_limit_bytes=63 << 20
        ),
    )(queries, keys, values, cache_keys, cache_values, levels, first_span, level_gate)


def solution(mesh):
    tokens = P(("span", "head"), None)
    placed = (
        tokens, tokens, tokens, P("span", "head"), P("span", "head"), P(), P(), P(None, "head"),
    )
    return jax.shard_map(shards, mesh=mesh, in_specs=placed, out_specs=tokens, check_vma=False)
```

```python
import functools
import math

import jax
import jax.numpy as jnp
from jax import lax
from jax.experimental import pallas as pl
from jax.experimental.pallas import tpu as pltpu
from jax.sharding import PartitionSpec as P

HD = 128
CL = 512
NX, NZ, NH = 4, 16, 8
NR = 4
J = 3
ROWS = 128
WIDTH = J * HD
TOK = 16
QS = NX * ROWS
LOW = -3.0e38
SCALE = HD**-0.5 * math.log2(math.e)
BF = jnp.bfloat16
F32 = jnp.float32
MESH = pl.DeviceIdType.MESH


def kernel(
    q_in, k_in, v_in, ck_in, cv_in, levels_in, first_in, gate_in, out,
    levels, first, kb, vt, cvv, gate, q_all, k_all, v_all, qx, qt, acc, m_st, l_st,
    cq, ck2, cv2, o_send, o_cur, p_send, p_rec, gate_cols,
    ring_s, ring_r, y_s, y_r, x_s, x_r, c_s, c_r, oc_s, oc_r, p_s, p_r, loc, fetch,
):
    s = lax.axis_index("span")
    h = lax.axis_index("head")
    x = s // NZ
    z = s % NZ
    zq = z // NR
    r = z % NR
    core = h % 2

    def at(xx, zz):
        return xx * NZ + zz

    right = at(x, (z + 1) % NZ)
    left = at(x, (z + NZ - 1) % NZ)

    def remote(src, dst, send, recv, span, head):
        return pltpu.make_async_remote_copy(
            src_ref=src, dst_ref=dst, send_sem=send, recv_sem=recv,
            device_id=(span, head), device_id_type=MESH,
        )

    barrier = pltpu.get_barrier_semaphore()
    for n in (right, left):
        pl.semaphore_signal(barrier, inc=1, device_id=(n, h), device_id_type=MESH)
    for o in range(1, NR):
        pl.semaphore_signal(
            barrier, inc=1, device_id=(at(x, zq * NR + (r + o) % NR), h), device_id_type=MESH
        )
    for o in range(1, NX):
        pl.semaphore_signal(barrier, inc=1, device_id=(at((x + o) % NX, z), h), device_id_type=MESH)
    for o in range(1, NH):
        pl.semaphore_signal(barrier, inc=1, device_id=(s, (h + o) % NH), device_id_type=MESH)

    fetch_v = pltpu.make_async_copy(cv_in, cvv, fetch.at[0])
    fetch_v.start()
    pl.semaphore_wait(barrier, 2 + NR - 1 + NX - 1 + NH - 1)

    def ring(d, kv, c, t):
        buf, half = ((kb, ROWS // 2), (vt, WIDTH // 2))[kv]
        rows = pl.ds(c * half, half)
        if d == 0:
            src, dst, n = t - 1, t, right
        else:
            src, dst, n = (NZ + 1 - t) % NZ, NZ - t, left
        source = ck_in.at[rows] if t == 1 and kv == 0 else buf.at[src, rows]
        return remote(source, buf.at[dst, rows], ring_s.at[d, kv, c, t], ring_r.at[d, kv, c, t], n, h)

    halves = [(kv, c) for kv in (0, 1) for c in (0, 1)]
    fresh = ((q_in, q_all), (k_in, k_all), (v_in, v_all))

    def to_heads(i, o):
        src, dst = fresh[i]
        n = (h + o) % NH
        return remote(
            src.at[:, pl.ds(pl.multiple_of(n * WIDTH, HD), WIDTH)],
            dst.at[pl.ds(pl.multiple_of(h * TOK, TOK), TOK), :],
            y_s.at[i, o], y_r.at[i, o], s, n,
        )

    def own_heads(i):
        src, dst = fresh[i]
        return pltpu.make_async_copy(
            src.at[:, pl.ds(pl.multiple_of(h * WIDTH, HD), WIDTH)],
            dst.at[pl.ds(pl.multiple_of(h * TOK, TOK), TOK), :],
            loc.at[i],
        )

    operands = (
        (cv_in, cvv), (ck_in, kb.at[0]), (gate_in, gate), (levels_in, levels), (first_in, first),
    )
    fetched = [pltpu.make_async_copy(a, b, fetch.at[i]) for i, (a, b) in enumerate(operands)]

    def send_heads(i):
        own_heads(i).start()
        for o in range(1, NH):
            to_heads(i, o).start()

    for c in (0, 1):
        for d in (0, 1):
            ring(d, 0, c, 1).start()
    for copy in fetched[1:]:
        copy.start()
    send_heads(0)
    fetched[0].wait()
    for j in range(J):
        vt[0, j * HD : (j + 1) * HD, :] = cvv[:, j * HD : (j + 1) * HD].T
    for c in (0, 1):
        for d in (0, 1):
            ring(d, 1, c, 1).start()
    send_heads(1)
    send_heads(2)

    def heads_arrived(i):
        own_heads(i).wait()
        for o in range(1, NH):
            to_heads(i, o).wait_recv()

    def to_row(o):
        return remote(q_all, qx.at[x], x_s.at[o], x_r.at[o], at((x + o) % NX, z), h)

    mine = r - core
    takes = (mine >= 0) & (mine < J)

    def to_taker(i, o):
        n = (r + o) % NR
        j = jnp.clip(n - core, 0, J - 1)
        src = (q_all, k_all, v_all)[i].at[:, pl.ds(pl.multiple_of(j * HD, HD), HD)]
        dst = (cq, ck2, cv2)[i].at[r]
        return remote(src, dst, c_s.at[i, o], c_r.at[i, o], at(x, zq * NR + n), h)

    def own_taken(i):
        j = jnp.clip(mine, 0, J - 1)
        src = (q_all, k_all, v_all)[i].at[:, pl.ds(pl.multiple_of(j * HD, HD), HD)]
        return pltpu.make_async_copy(src, (cq, ck2, cv2)[i].at[r], loc.at[3 + i])

    def sends_to(o):
        n = (r + o) % NR
        return (n - core >= 0) & (n - core < J)

    def forward(t, *work):
        for n, (kv, c) in enumerate(halves):
            for d in (0, 1):
                ring(d, kv, c, t).wait_recv()
                if t < 7:
                    ring(d, kv, c, t + 1).start()
            if t == 7:
                last(kv, c, "start")
            for item in work[n : n + 1]:
                item()

    def sent(t):
        for kv, c in halves:
            for d in (0, 1):
                ring(d, kv, c, t).wait_send()

    def last(kv, c, what):
        getattr(ring(kv, kv, c, 8), what)()

    own_q = pltpu.make_async_copy(q_all, qx.at[x], loc.at[0])

    def share_queries():
        heads_arrived(0)
        for o in range(1, NX):
            to_row(o).start()
        own_q.start()

    def share_current():
        heads_arrived(2)
        for o in range(1, NR):

            @pl.when(sends_to(o))
            def _():
                for i in range(3):
                    to_taker(i, o).start()

        @pl.when(takes)
        def _():
            for i in range(3):
                own_taken(i).start()

    def clear():
        acc[...] = jnp.zeros_like(acc)
        m_st[...] = jnp.full_like(m_st, LOW)
        l_st[...] = jnp.zeros_like(l_st)
        for i in range(1, NX):

            @pl.when(i > x)
            def _():
                p_rec[i] = jnp.zeros((NH, TOK, WIDTH + HD), BF)

    forward(1)
    share_queries()
    heads_arrived(1)
    share_current()
    clear()

    def spread_gate(i):
        if i == 0:
            for n in range(2, 5):
                fetched[n].wait()
        level_row = lax.broadcasted_iota(jnp.int32, (16, WIDTH), 0)
        gate_row = jnp.sum(
            jnp.where(level_row == levels[i * NR + zq], gate[...], 0.0), axis=0, keepdims=True
        )
        for j in range(J):
            gate_cols[i, j] = jnp.broadcast_to(gate_row[:, j * HD : (j + 1) * HD], (ROWS, HD)).T

    forward(2, *[functools.partial(spread_gate, i) for i in range(NX)])

    fetched[1].wait()

    def turn_queries(j):
        if j == 0:
            own_q.wait()
            for o in range(1, NX):
                to_row(o).wait_recv()
        for i in range(NX):
            qt[j, :, i * ROWS : (i + 1) * ROWS] = qx[i, :, j * HD : (j + 1) * HD].T

    forward(3, *[functools.partial(turn_queries, j) for j in range(J)])

    lane_row = lax.broadcasted_iota(jnp.int32, (1, QS), 1) // ROWS
    q_span = lane_row * NR + zq
    q_first = jnp.zeros((1, QS), jnp.int32)
    for i in range(NX):
        q_first = jnp.where(lane_row == i, first[i * NR + zq], q_first)

    def sees(slot):
        c = x * NR + ((z - slot + NZ) % NZ) // NR
        return (q_first <= c) & (q_span > c)

    def attend_head(j, slots, lanes=slice(0, QS)):
        cols = slice(j * HD, (j + 1) * HD)
        query = qt[j, :, lanes]
        seen = [sees(i)[:, lanes] for i in slots]
        scores = [jnp.dot(kb[i, :, cols], query, preferred_element_type=F32) for i in slots]
        old = m_st[j, :, lanes]
        peak = old
        for see, score in zip(seen, scores):
            peak = jnp.maximum(peak, jnp.where(see, jnp.max(score, axis=0, keepdims=True) * SCALE, LOW))
        shrink = jnp.exp2(old - peak)
        total = l_st[j, :, lanes] * shrink
        product = acc[j, :, lanes] * shrink
        for i, see, score in zip(slots, seen, scores):
            weight = jnp.exp2(score * SCALE - jnp.where(see, peak, jnp.inf))
            total += jnp.sum(weight, axis=0, keepdims=True)
            product += jnp.dot(vt[i, cols, :], weight.astype(BF), preferred_element_type=F32)
        m_st[j, :, lanes] = peak
        l_st[j, :, lanes] = total
        acc[j, :, lanes] = product

    def head(j, *slots):
        return functools.partial(attend_head, j, slots)

    def both(*items):
        def run():
            for item in items:
                item()

        return run

    def packed(part, peak, total):
        row = lax.broadcasted_iota(jnp.int32, (16, ROWS), 0)
        tile = jnp.zeros((16, ROWS), F32)
        for first_row, value in ((0, peak), (3, total)):
            for i in range(3):
                piece = value.astype(BF).astype(F32)
                tile = jnp.where(row == first_row + i, piece, tile)
                value = value - piece
        return jnp.concatenate([part, tile], axis=0).astype(BF)

    def unpacked(block):
        tile = block[HD:].astype(F32)
        return block[:HD].astype(F32), tile[0:1] + tile[1:2] + tile[2:3], tile[3:4] + tile[4:5] + tile[5:6]

    def to_rows_of_span(o):
        n = (r + o) % NR
        j = jnp.clip(mine, 0, J - 1)
        return remote(o_send.at[n], o_cur.at[j], oc_s.at[o], oc_r.at[o], at(x, zq * NR + n), h)

    own_part = pltpu.make_async_copy(o_send.at[r], o_cur.at[jnp.clip(mine, 0, J - 1)], loc.at[3])

    def current(n):
        @pl.when(takes)
        def _():
            if n == 0:
                for i in range(3):
                    own_taken(i).wait()
                    for o in range(1, NR):
                        to_taker(i, o).wait_recv()
            keys = ck2[...].reshape(CL, HD)
            scores = jnp.dot(keys, cq[n].T, preferred_element_type=F32)
            peak = jnp.max(scores, axis=0, keepdims=True) * SCALE
            weights = jnp.exp2(scores * SCALE - peak)
            total = jnp.sum(weights, axis=0, keepdims=True)
            value = jnp.concatenate([cv2[i].T for i in range(NR)], axis=1)
            part = jnp.dot(value, weights.astype(BF), preferred_element_type=F32) * (1.0 / total)
            o_send[n] = packed(part, peak, total)
            if n == NR - 1:
                own_part.start()
                for o in range(1, NR):
                    to_rows_of_span(o).start()

    def current_arrived():
        @pl.when(takes)
        def _():
            own_part.wait()

        for o in range(1, NR):
            n = (r - o + NR) % NR

            @pl.when((n - core >= 0) & (n - core < J))
            def _():
                remote(
                    o_send.at[0], o_cur.at[jnp.clip(n - core, 0, J - 1)], oc_s.at[o], oc_r.at[o],
                    at(x, zq * NR + n), h,
                ).wait_recv()

    def merge_current(j):
        part, peak, total = unpacked(o_cur[j])
        lanes = pl.ds(pl.multiple_of(x * ROWS, ROWS), ROWS)
        old = m_st[j, :, lanes]
        new = jnp.maximum(old, peak)
        shrink, share = jnp.exp2(old - new), total * jnp.exp2(peak - new)
        m_st[j, :, lanes] = new
        l_st[j, :, lanes] = l_st[j, :, lanes] * shrink + share
        acc[j, :, lanes] = acc[j, :, lanes] * shrink + part * share

    def sent_entry():
        for i in range(3):
            for o in range(1, NH):
                to_heads(i, o).wait_send()
        for o in range(1, NX):
            to_row(o).wait_send()

    def sent_current():
        for o in range(1, NR):

            @pl.when(sends_to(o))
            def _():
                for i in range(3):
                    to_taker(i, o).wait_send()

        @pl.when(takes)
        def _():
            for o in range(1, NR):
                to_rows_of_span(o).wait_send()

    cur = [functools.partial(current, n) for n in range(NR)]
    merge = [functools.partial(merge_current, j) for j in range(J)]
    sent(1)
    forward(4, head(0, 0, 1, 15), head(1, 0, 1, 15), head(2, 0, 1, 15), cur[0])
    sent(2)
    forward(5, cur[1], cur[2], cur[3], both(head(0, 2, 14), sent_entry))
    sent(3)
    forward(
        6,
        both(head(1, 2, 14), head(2, 2, 14)), both(head(0, 3, 13), head(1, 3, 13)),
        both(head(2, 3, 13), head(0, 4, 12)), both(head(1, 4, 12), head(2, 4, 12)),
    )
    sent(4)
    forward(
        7,
        both(head(0, 5, 11), head(1, 5, 11)), both(head(2, 5, 11), current_arrived, sent_current),
        both(head(0, 6, 10), head(1, 6, 10)), both(head(2, 6, 10), *merge),
    )
    for j in range(J):
        attend_head(j, (7, 9))
    sent(5)
    sent(6)

    def to_owner(i, n):
        return remote(
            p_send.at[i, pl.ds(pl.multiple_of(n * TOK, TOK), TOK), :], p_rec.at[x, h],
            p_s.at[i, n], p_r.at[x, h], at(i, z), n,
        )

    def from_part(i, n):
        return remote(p_send.at[i, pl.ds(0, TOK), :], p_rec.at[i, n], p_s.at[i, n], p_r.at[i, n], at(i, z), n)

    own_tokens = pltpu.make_async_copy(
        p_send.at[x, pl.ds(pl.multiple_of(h * TOK, TOK), TOK), :], p_rec.at[x, h], loc.at[0]
    )

    def logs(i):
        lanes = slice(i * ROWS, (i + 1) * ROWS)
        row = lax.broadcasted_iota(jnp.int32, (ROWS, ROWS), 0)
        tile = jnp.zeros((ROWS, ROWS), F32)
        for j in range(J):
            total = l_st[j][:, lanes]
            value = jnp.where(
                total > 0.0,
                m_st[j][:, lanes] + jnp.log(jnp.where(total > 0.0, total, 1.0)) * math.log2(math.e),
                LOW,
            )
            for n in range(3):
                piece = value.astype(BF).astype(F32)
                tile = jnp.where(row == 3 * n + j, piece, tile)
                value = value - piece
        return tile.T

    for kv, c in halves:
        last(kv, c, "wait_recv")
    def finish(i):
        lanes = slice(i * ROWS, (i + 1) * ROWS)
        for j in range(J):
            attend_head(j, (8,), lanes)
            total = l_st[j][:, lanes]
            part = acc[j][:, lanes] * (1.0 / jnp.where(total > 0.0, total, 1.0)) * gate_cols[i, j]
            p_send[i, :, j * HD : (j + 1) * HD] = part.astype(BF).T
        p_send[i, :, WIDTH:] = logs(i).astype(BF)
        for o in range(1, NH):
            to_owner(i, (h + o) % NH).start()

    for i in (1, 3, 2):

        @pl.when(i > x)
        def _():
            finish(i)
            to_owner(i, h).start()

    for i in range(NX):

        @pl.when(i == x)
        def _():
            finish(i)
            own_tokens.start()

    sent(7)
    for kv, c in halves:
        last(kv, c, "wait_send")
    for i in range(NX):
        for n in range(NH):

            @pl.when((i > x) | ((i == x) & (n != h)))
            def _():
                to_owner(i, n).wait_send()

    own_tokens.wait()
    for n in range(NH):
        for i in range(NX):

            @pl.when((i < x) | ((i == x) & (n != h)))
            def _():
                from_part(i, n).wait_recv()

        marks = []
        for i in range(NX):
            tile = p_rec[i, n, :, WIDTH:].astype(F32)
            mark = tile + pltpu.roll(tile, ROWS - 3, 1) + pltpu.roll(tile, ROWS - 6, 1)
            marks.append(jnp.where(i <= x, mark, LOW))
        peak = functools.reduce(jnp.maximum, marks)
        shares = [jnp.exp2(m - peak) for m in marks]
        scale = 1.0 / functools.reduce(jnp.add, shares)
        shares = [w * scale for w in shares]
        for j in range(J):
            cols = slice(j * HD, (j + 1) * HD)
            mixed = functools.reduce(
                jnp.add, [w[:, j : j + 1] * p_rec[i, n, :, cols].astype(F32) for i, w in enumerate(shares)]
            )
            out[:, n * WIDTH + j * HD : n * WIDTH + (j + 1) * HD] = mixed.astype(BF)


def shards(queries, keys, values, cache_keys, cache_values, levels, first_span, level_gate):
    hbm = pl.BlockSpec(memory_space=pltpu.HBM)
    dma = pltpu.SemaphoreType.DMA
    return pl.pallas_call(
        kernel,
        out_shape=pltpu.VMEM((TOK, NH * WIDTH), BF),
        in_specs=[hbm] * 8,
        out_specs=pl.BlockSpec(memory_space=pltpu.VMEM),
        scratch_shapes=[
            pltpu.SMEM((16,), jnp.int32),
            pltpu.SMEM((16,), jnp.int32),
            pltpu.VMEM((NZ, ROWS, WIDTH), BF),
            pltpu.VMEM((NZ, WIDTH, ROWS), BF),
            pltpu.VMEM((ROWS, WIDTH), BF),
            pltpu.VMEM((16, WIDTH), F32),
            pltpu.VMEM((ROWS, WIDTH), BF),
            pltpu.VMEM((ROWS, WIDTH), BF),
            pltpu.VMEM((ROWS, WIDTH), BF),
            pltpu.VMEM((NX, ROWS, WIDTH), BF),
            pltpu.VMEM((J, HD, QS), BF),
            pltpu.VMEM((J, HD, QS), F32),
            pltpu.VMEM((J, 1, QS), F32),
            pltpu.VMEM((J, 1, QS), F32),
            pltpu.VMEM((NR, ROWS, HD), BF),
            pltpu.VMEM((NR, ROWS, HD), BF),
            pltpu.VMEM((NR, ROWS, HD), BF),
            pltpu.VMEM((NR, HD + 16, ROWS), BF),
            pltpu.VMEM((J, HD + 16, ROWS), BF),
            pltpu.VMEM((NX, ROWS, WIDTH + HD), BF),
            pltpu.VMEM((NX, NH, TOK, WIDTH + HD), BF),
            pltpu.VMEM((NX, J, HD, ROWS), F32),
            dma((2, 2, 2, 9)),
            dma((2, 2, 2, 9)),
            dma((3, NH)),
            dma((3, NH)),
            dma((NX,)),
            dma((NX,)),
            dma((3, NR)),
            dma((3, NR)),
            dma((NR,)),
            dma((NR,)),
            dma((NX, NH)),
            dma((NX, NH)),
            dma((6,)),
            dma((5,)),
        ],
        compiler_params=pltpu.CompilerParams(
            collective_id=0, has_side_effects=True, vmem_limit_bytes=63 << 20
        ),
    )(queries, keys, values, cache_keys, cache_values, levels, first_span, level_gate)


def solution(mesh):
    tokens = P(("span", "head"), None)
    placed = (
        tokens, tokens, tokens, P("span", "head"), P("span", "head"), P(), P(), P(None, "head"),
    )
    return jax.shard_map(shards, mesh=mesh, in_specs=placed, out_specs=tokens, check_vma=False)
```

```python
import functools
import math

import jax
import jax.numpy as jnp
from jax import lax
from jax.experimental import pallas as pl
from jax.experimental.pallas import tpu as pltpu
from jax.sharding import PartitionSpec as P

HD = 128
CL = 512
NX, NZ, NH = 4, 16, 8
NR = 4
J = 3
ROWS = 128
WIDTH = J * HD
TOK = 16
QS = NX * ROWS
LOW = -3.0e38
SCALE = HD**-0.5 * math.log2(math.e)
BF = jnp.bfloat16
F32 = jnp.float32
MESH = pl.DeviceIdType.MESH


def kernel(
    q_in, k_in, v_in, ck_in, cv_in, levels_in, first_in, gate_in, out,
    levels, first, kb, vt, cvv, gate, q_all, k_all, v_all, qx, qt, acc, m_st, l_st,
    cq, ck2, cv2, o_send, o_cur, p_send, p_rec, gate_cols,
    ring_s, ring_r, y_s, y_r, x_s, x_r, c_s, c_r, oc_s, oc_r, p_s, p_r, loc, fetch,
):
    s = lax.axis_index("span")
    h = lax.axis_index("head")
    x = s // NZ
    z = s % NZ
    zq = z // NR
    r = z % NR
    core = h % 2

    def at(xx, zz):
        return xx * NZ + zz

    right = at(x, (z + 1) % NZ)
    left = at(x, (z + NZ - 1) % NZ)

    def remote(src, dst, send, recv, span, head):
        return pltpu.make_async_remote_copy(
            src_ref=src, dst_ref=dst, send_sem=send, recv_sem=recv,
            device_id=(span, head), device_id_type=MESH,
        )

    barrier = pltpu.get_barrier_semaphore()
    for n in (right, left):
        pl.semaphore_signal(barrier, inc=1, device_id=(n, h), device_id_type=MESH)
    for o in range(1, NR):
        pl.semaphore_signal(
            barrier, inc=1, device_id=(at(x, zq * NR + (r + o) % NR), h), device_id_type=MESH
        )
    for o in range(1, NX):
        pl.semaphore_signal(barrier, inc=1, device_id=(at((x + o) % NX, z), h), device_id_type=MESH)
    for o in range(1, NH):
        pl.semaphore_signal(barrier, inc=1, device_id=(s, (h + o) % NH), device_id_type=MESH)

    fetch_v = pltpu.make_async_copy(cv_in, cvv, fetch.at[0])
    fetch_v.start()
    pl.semaphore_wait(barrier, 2 + NR - 1 + NX - 1 + NH - 1)

    def ring(d, kv, c, t):
        buf, half = ((kb, ROWS // 2), (vt, WIDTH // 2))[kv]
        rows = pl.ds(c * half, half)
        if d == 0:
            src, dst, n = t - 1, t, right
        else:
            src, dst, n = (NZ + 1 - t) % NZ, NZ - t, left
        source = ck_in.at[rows] if t == 1 and kv == 0 else buf.at[src, rows]
        return remote(source, buf.at[dst, rows], ring_s.at[d, kv, c, t], ring_r.at[d, kv, c, t], n, h)

    halves = [(kv, c) for kv in (0, 1) for c in (0, 1)]
    fresh = ((q_in, q_all), (k_in, k_all), (v_in, v_all))

    def to_heads(i, o):
        src, dst = fresh[i]
        n = (h + o) % NH
        return remote(
            src.at[:, pl.ds(pl.multiple_of(n * WIDTH, HD), WIDTH)],
            dst.at[pl.ds(pl.multiple_of(h * TOK, TOK), TOK), :],
            y_s.at[i, o], y_r.at[i, o], s, n,
        )

    def own_heads(i):
        src, dst = fresh[i]
        return pltpu.make_async_copy(
            src.at[:, pl.ds(pl.multiple_of(h * WIDTH, HD), WIDTH)],
            dst.at[pl.ds(pl.multiple_of(h * TOK, TOK), TOK), :],
            loc.at[i],
        )

    operands = (
        (cv_in, cvv), (ck_in, kb.at[0]), (gate_in, gate), (levels_in, levels), (first_in, first),
    )
    fetched = [pltpu.make_async_copy(a, b, fetch.at[i]) for i, (a, b) in enumerate(operands)]

    def send_heads(i):
        own_heads(i).start()
        for o in range(1, NH):
            to_heads(i, o).start()

    for c in (0, 1):
        for d in (0, 1):
            ring(d, 0, c, 1).start()
    for copy in fetched[1:]:
        copy.start()
    send_heads(0)
    fetched[0].wait()
    for j in range(J):
        vt[0, j * HD : (j + 1) * HD, :] = cvv[:, j * HD : (j + 1) * HD].T
    for c in (0, 1):
        for d in (0, 1):
            ring(d, 1, c, 1).start()
    send_heads(1)
    send_heads(2)

    def heads_arrived(i):
        own_heads(i).wait()
        for o in range(1, NH):
            to_heads(i, o).wait_recv()

    def to_row(o):
        return remote(q_all, qx.at[x], x_s.at[o], x_r.at[o], at((x + o) % NX, z), h)

    mine = r - core
    takes = (mine >= 0) & (mine < J)

    def to_taker(i, o):
        n = (r + o) % NR
        j = jnp.clip(n - core, 0, J - 1)
        src = (q_all, k_all, v_all)[i].at[:, pl.ds(pl.multiple_of(j * HD, HD), HD)]
        dst = (cq, ck2, cv2)[i].at[r]
        return remote(src, dst, c_s.at[i, o], c_r.at[i, o], at(x, zq * NR + n), h)

    def own_taken(i):
        j = jnp.clip(mine, 0, J - 1)
        src = (q_all, k_all, v_all)[i].at[:, pl.ds(pl.multiple_of(j * HD, HD), HD)]
        return pltpu.make_async_copy(src, (cq, ck2, cv2)[i].at[r], loc.at[3 + i])

    def sends_to(o):
        n = (r + o) % NR
        return (n - core >= 0) & (n - core < J)

    def forward(t, *work):
        for n, (kv, c) in enumerate(halves):
            for d in (0, 1):
                ring(d, kv, c, t).wait_recv()
                if t < 7:
                    ring(d, kv, c, t + 1).start()
            if t == 7:
                last(kv, c, "start")
            for item in work[n : n + 1]:
                item()

    def sent(t):
        for kv, c in halves:
            for d in (0, 1):
                ring(d, kv, c, t).wait_send()

    def last(kv, c, what):
        getattr(ring(kv, kv, c, 8), what)()

    own_q = pltpu.make_async_copy(q_all, qx.at[x], loc.at[0])

    def share_queries():
        heads_arrived(0)
        for o in range(1, NX):
            to_row(o).start()
        own_q.start()

    def share_current():
        heads_arrived(2)
        for o in range(1, NR):

            @pl.when(sends_to(o))
            def _():
                for i in range(3):
                    to_taker(i, o).start()

        @pl.when(takes)
        def _():
            for i in range(3):
                own_taken(i).start()

    def clear():
        acc[...] = jnp.zeros_like(acc)
        m_st[...] = jnp.full_like(m_st, LOW)
        l_st[...] = jnp.zeros_like(l_st)
        for i in range(1, NX):

            @pl.when(i > x)
            def _():
                p_rec[i] = jnp.zeros((NH, TOK, WIDTH + HD), BF)

    forward(1)
    share_queries()
    heads_arrived(1)
    share_current()
    clear()

    def spread_gate(i):
        if i == 0:
            for n in range(2, 5):
                fetched[n].wait()
        level_row = lax.broadcasted_iota(jnp.int32, (16, WIDTH), 0)
        gate_row = jnp.sum(
            jnp.where(level_row == levels[i * NR + zq], gate[...], 0.0), axis=0, keepdims=True
        )
        for j in range(J):
            gate_cols[i, j] = jnp.broadcast_to(gate_row[:, j * HD : (j + 1) * HD], (ROWS, HD)).T

    forward(2, *[functools.partial(spread_gate, i) for i in range(NX)])

    fetched[1].wait()

    def turn_queries(j):
        if j == 0:
            own_q.wait()
            for o in range(1, NX):
                to_row(o).wait_recv()
        for i in range(NX):
            qt[j, :, i * ROWS : (i + 1) * ROWS] = qx[i, :, j * HD : (j + 1) * HD].T

    forward(3, *[functools.partial(turn_queries, j) for j in range(J)])

    lane_row = lax.broadcasted_iota(jnp.int32, (1, QS), 1) // ROWS
    q_span = lane_row * NR + zq
    q_first = jnp.zeros((1, QS), jnp.int32)
    for i in range(NX):
        q_first = jnp.where(lane_row == i, first[i * NR + zq], q_first)

    def sees(slot):
        c = x * NR + ((z - slot + NZ) % NZ) // NR
        return (q_first <= c) & (q_span > c)

    def attend_head(j, slots, lanes=slice(0, QS)):
        cols = slice(j * HD, (j + 1) * HD)
        query = qt[j, :, lanes]
        seen = [sees(i)[:, lanes] for i in slots]
        scores = [jnp.dot(kb[i, :, cols], query, preferred_element_type=F32) for i in slots]
        old = m_st[j, :, lanes]
        peak = old
        for see, score in zip(seen, scores):
            peak = jnp.maximum(peak, jnp.where(see, jnp.max(score, axis=0, keepdims=True) * SCALE, LOW))
        shrink = jnp.exp2(old - peak)
        total = l_st[j, :, lanes] * shrink
        product = acc[j, :, lanes] * shrink
        for i, see, score in zip(slots, seen, scores):
            weight = jnp.exp2(jnp.where(see, score * SCALE - peak, -jnp.inf))
            total += jnp.sum(weight, axis=0, keepdims=True)
            product += jnp.dot(vt[i, cols, :], weight.astype(BF), preferred_element_type=F32)
        m_st[j, :, lanes] = peak
        l_st[j, :, lanes] = total
        acc[j, :, lanes] = product

    def head(j, *slots):
        return functools.partial(attend_head, j, slots)

    def both(*items):
        def run():
            for item in items:
                item()

        return run

    def packed(part, peak, total):
        row = lax.broadcasted_iota(jnp.int32, (16, ROWS), 0)
        tile = jnp.zeros((16, ROWS), F32)
        for first_row, value in ((0, peak), (3, total)):
            for i in range(3):
                piece = value.astype(BF).astype(F32)
                tile = jnp.where(row == first_row + i, piece, tile)
                value = value - piece
        return jnp.concatenate([part, tile], axis=0).astype(BF)

    def unpacked(block):
        tile = block[HD:].astype(F32)
        return block[:HD].astype(F32), tile[0:1] + tile[1:2] + tile[2:3], tile[3:4] + tile[4:5] + tile[5:6]

    def to_rows_of_span(o):
        n = (r + o) % NR
        j = jnp.clip(mine, 0, J - 1)
        return remote(o_send.at[n], o_cur.at[j], oc_s.at[o], oc_r.at[o], at(x, zq * NR + n), h)

    own_part = pltpu.make_async_copy(o_send.at[r], o_cur.at[jnp.clip(mine, 0, J - 1)], loc.at[3])

    def current(n):
        @pl.when(takes)
        def _():
            if n == 0:
                for i in range(3):
                    own_taken(i).wait()
                    for o in range(1, NR):
                        to_taker(i, o).wait_recv()
            keys = ck2[...].reshape(CL, HD)
            scores = jnp.dot(keys, cq[n].T, preferred_element_type=F32)
            peak = jnp.max(scores, axis=0, keepdims=True) * SCALE
            weights = jnp.exp2(scores * SCALE - peak)
            total = jnp.sum(weights, axis=0, keepdims=True)
            value = jnp.concatenate([cv2[i].T for i in range(NR)], axis=1)
            part = jnp.dot(value, weights.astype(BF), preferred_element_type=F32) * (1.0 / total)
            o_send[n] = packed(part, peak, total)
            if n == NR - 1:
                own_part.start()
                for o in range(1, NR):
                    to_rows_of_span(o).start()

    def current_arrived():
        @pl.when(takes)
        def _():
            own_part.wait()

        for o in range(1, NR):
            n = (r - o + NR) % NR

            @pl.when((n - core >= 0) & (n - core < J))
            def _():
                remote(
                    o_send.at[0], o_cur.at[jnp.clip(n - core, 0, J - 1)], oc_s.at[o], oc_r.at[o],
                    at(x, zq * NR + n), h,
                ).wait_recv()

    def merge_current(j):
        part, peak, total = unpacked(o_cur[j])
        lanes = pl.ds(pl.multiple_of(x * ROWS, ROWS), ROWS)
        old = m_st[j, :, lanes]
        new = jnp.maximum(old, peak)
        shrink, share = jnp.exp2(old - new), total * jnp.exp2(peak - new)
        m_st[j, :, lanes] = new
        l_st[j, :, lanes] = l_st[j, :, lanes] * shrink + share
        acc[j, :, lanes] = acc[j, :, lanes] * shrink + part * share

    def sent_entry():
        for i in range(3):
            for o in range(1, NH):
                to_heads(i, o).wait_send()
        for o in range(1, NX):
            to_row(o).wait_send()

    def sent_current():
        for o in range(1, NR):

            @pl.when(sends_to(o))
            def _():
                for i in range(3):
                    to_taker(i, o).wait_send()

        @pl.when(takes)
        def _():
            for o in range(1, NR):
                to_rows_of_span(o).wait_send()

    cur = [functools.partial(current, n) for n in range(NR)]
    merge = [functools.partial(merge_current, j) for j in range(J)]
    sent(1)
    forward(4, head(0, 0, 1, 15), head(1, 0, 1, 15), head(2, 0, 1, 15), cur[0])
    sent(2)
    forward(5, cur[1], cur[2], cur[3], both(head(0, 2, 14), sent_entry))
    sent(3)
    forward(
        6,
        both(head(1, 2, 14), head(2, 2, 14)), both(head(0, 3, 13), head(1, 3, 13)),
        both(head(2, 3, 13), head(0, 4, 12)), both(head(1, 4, 12), head(2, 4, 12)),
    )
    sent(4)
    forward(
        7,
        both(head(0, 5, 11), head(1, 5, 11)), both(head(2, 5, 11), current_arrived, sent_current),
        both(head(0, 6, 10), head(1, 6, 10)), both(head(2, 6, 10), *merge),
    )
    for j in range(J):
        attend_head(j, (7, 9))
    sent(5)
    sent(6)

    def to_owner(i, n):
        return remote(
            p_send.at[i, pl.ds(pl.multiple_of(n * TOK, TOK), TOK), :], p_rec.at[x, h],
            p_s.at[i, n], p_r.at[x, h], at(i, z), n,
        )

    def from_part(i, n):
        return remote(p_send.at[i, pl.ds(0, TOK), :], p_rec.at[i, n], p_s.at[i, n], p_r.at[i, n], at(i, z), n)

    own_tokens = pltpu.make_async_copy(
        p_send.at[x, pl.ds(pl.multiple_of(h * TOK, TOK), TOK), :], p_rec.at[x, h], loc.at[0]
    )

    def logs(i):
        lanes = slice(i * ROWS, (i + 1) * ROWS)
        row = lax.broadcasted_iota(jnp.int32, (ROWS, ROWS), 0)
        tile = jnp.zeros((ROWS, ROWS), F32)
        for j in range(J):
            total = l_st[j][:, lanes]
            value = jnp.where(
                total > 0.0,
                m_st[j][:, lanes] + jnp.log(jnp.where(total > 0.0, total, 1.0)) * math.log2(math.e),
                LOW,
            )
            for n in range(3):
                piece = value.astype(BF).astype(F32)
                tile = jnp.where(row == 3 * n + j, piece, tile)
                value = value - piece
        return tile.T

    for kv, c in halves:
        last(kv, c, "wait_recv")
    def finish(i):
        lanes = slice(i * ROWS, (i + 1) * ROWS)
        for j in range(J):
            attend_head(j, (8,), lanes)
            total = l_st[j][:, lanes]
            part = acc[j][:, lanes] * (1.0 / jnp.where(total > 0.0, total, 1.0)) * gate_cols[i, j]
            p_send[i, :, j * HD : (j + 1) * HD] = part.astype(BF).T
        p_send[i, :, WIDTH:] = logs(i).astype(BF)
        for o in range(1, NH):
            to_owner(i, (h + o) % NH).start()

    for i in (1, 3, 2):

        @pl.when(i > x)
        def _():
            finish(i)
            to_owner(i, h).start()

    for i in range(NX):

        @pl.when(i == x)
        def _():
            finish(i)
            own_tokens.start()

    sent(7)
    for kv, c in halves:
        last(kv, c, "wait_send")
    for i in range(NX):
        for n in range(NH):

            @pl.when((i > x) | ((i == x) & (n != h)))
            def _():
                to_owner(i, n).wait_send()

    own_tokens.wait()
    for n in range(NH):
        for i in range(NX):

            @pl.when((i < x) | ((i == x) & (n != h)))
            def _():
                from_part(i, n).wait_recv()

        marks = []
        for i in range(NX):
            tile = p_rec[i, n, :, WIDTH:].astype(F32)
            mark = tile + pltpu.roll(tile, ROWS - 3, 1) + pltpu.roll(tile, ROWS - 6, 1)
            marks.append(jnp.where(i <= x, mark, LOW))
        peak = functools.reduce(jnp.maximum, marks)
        shares = [jnp.exp2(m - peak) for m in marks]
        scale = 1.0 / functools.reduce(jnp.add, shares)
        shares = [w * scale for w in shares]
        for j in range(J):
            cols = slice(j * HD, (j + 1) * HD)
            mixed = functools.reduce(
                jnp.add, [w[:, j : j + 1] * p_rec[i, n, :, cols].astype(F32) for i, w in enumerate(shares)]
            )
            out[:, n * WIDTH + j * HD : n * WIDTH + (j + 1) * HD] = mixed.astype(BF)


def shards(queries, keys, values, cache_keys, cache_values, levels, first_span, level_gate):
    hbm = pl.BlockSpec(memory_space=pltpu.HBM)
    dma = pltpu.SemaphoreType.DMA
    return pl.pallas_call(
        kernel,
        out_shape=pltpu.VMEM((TOK, NH * WIDTH), BF),
        in_specs=[hbm] * 8,
        out_specs=pl.BlockSpec(memory_space=pltpu.VMEM),
        scratch_shapes=[
            pltpu.SMEM((16,), jnp.int32),
            pltpu.SMEM((16,), jnp.int32),
            pltpu.VMEM((NZ, ROWS, WIDTH), BF),
            pltpu.VMEM((NZ, WIDTH, ROWS), BF),
            pltpu.VMEM((ROWS, WIDTH), BF),
            pltpu.VMEM((16, WIDTH), F32),
            pltpu.VMEM((ROWS, WIDTH), BF),
            pltpu.VMEM((ROWS, WIDTH), BF),
            pltpu.VMEM((ROWS, WIDTH), BF),
            pltpu.VMEM((NX, ROWS, WIDTH), BF),
            pltpu.VMEM((J, HD, QS), BF),
            pltpu.VMEM((J, HD, QS), F32),
            pltpu.VMEM((J, 1, QS), F32),
            pltpu.VMEM((J, 1, QS), F32),
            pltpu.VMEM((NR, ROWS, HD), BF),
            pltpu.VMEM((NR, ROWS, HD), BF),
            pltpu.VMEM((NR, ROWS, HD), BF),
            pltpu.VMEM((NR, HD + 16, ROWS), BF),
            pltpu.VMEM((J, HD + 16, ROWS), BF),
            pltpu.VMEM((NX, ROWS, WIDTH + HD), BF),
            pltpu.VMEM((NX, NH, TOK, WIDTH + HD), BF),
            pltpu.VMEM((NX, J, HD, ROWS), F32),
            dma((2, 2, 2, 9)),
            dma((2, 2, 2, 9)),
            dma((3, NH)),
            dma((3, NH)),
            dma((NX,)),
            dma((NX,)),
            dma((3, NR)),
            dma((3, NR)),
            dma((NR,)),
            dma((NR,)),
            dma((NX, NH)),
            dma((NX, NH)),
            dma((6,)),
            dma((5,)),
        ],
        compiler_params=pltpu.CompilerParams(
            collective_id=0, has_side_effects=True, vmem_limit_bytes=63 << 20
        ),
    )(queries, keys, values, cache_keys, cache_values, levels, first_span, level_gate)


def solution(mesh):
    tokens = P(("span", "head"), None)
    placed = (
        tokens, tokens, tokens, P("span", "head"), P("span", "head"), P(), P(), P(None, "head"),
    )
    return jax.shard_map(shards, mesh=mesh, in_specs=placed, out_specs=tokens, check_vma=False)
```
